512 devices in a mesh: section: 16 (over y, z_hi), replica: 4 (over x), tensor: 8 (over z_lo, core).
Axes of the slice: x: 4, y: 8, z: 8 (z_hi: 2, z_lo: 4; z = z_hi * 4 + z_lo), core: 2. Of those that a mesh axis runs over, the one named last changes fastest.
Arguments:
- act_log: bfloat16 [16, 1024, 5120], P('section', 'replica', 'tensor'), may hold values from -16 to 16
- grad_log: bfloat16 [16, 1024, 5120], P('section', 'replica', 'tensor'), may hold values from -16 to 16
- failed_section: int32 [16], replicated, may hold values from 0 to 15, each once
- live_tokens: int32 [4], replicated, may hold values from 1 to 256, 768 in all
- gate_weight: bfloat16 [5120, 13824], P('tensor', ('section', 'replica')), may hold values from -0.078125 to 0.078125
- up_weight: bfloat16 [5120, 13824], P('tensor', ('section', 'replica')), may hold values from -0.078125 to 0.078125
- down_weight: bfloat16 [13824, 5120], P(('section', 'replica'), 'tensor'), may hold values from -0.0546875 to 0.0546875
- norm_gain: bfloat16 [5120], P('tensor'), may hold values from 0.099609375 to 1.8984375
Outputs:
- d_input: bfloat16 [1024, 5120], P(('section', 'replica'), 'tensor')
- grad_gate: bfloat16 [5120, 13824], P('tensor', ('section', 'replica'))
- grad_up: bfloat16 [5120, 13824], P('tensor', ('section', 'replica'))
- grad_down: bfloat16 [13824, 5120], P(('section', 'replica'), 'tensor')
- grad_gain: float32 [5120], P('tensor')
The draws below stay inside these ranges and needn't reach their ends.
Inputs may be any that keep to these rules, and one draw needn't show every extreme that they name: `failed_section`: each section index appears exactly once. `live_tokens`: the entries sum to 768 and some micro-batch is full.
All inputs are finite; a program needn't handle non-finite values.
Results may differ from the reference program's by a relative error of at most 0.027.
Values may be sent and summed in bfloat16 or wider, within the bound.
No kernel may reach another device: no remote copies, remote signals or barrier semaphores. Data moves between devices by JAX's collectives and lax.ppermute only.
A program may use at most 64 MiB of HBM per device.

```python
import math
import jax
import jax.numpy as jnp
import numpy as np
from jax import lax

D = 5120
FF = 13824
TOK = 256
MICRO = 4
SECTIONS = 16
ROWS = 1024
N_TENSOR = 8


def draw_act_log(key, part):
    key = jax.random.fold_in(key, 11)
    base_key, scale_key = jax.random.split(key)
    column = jnp.arange(D, dtype=jnp.float32) / D
    spread = jnp.exp(jnp.log(3.0) * column + jax.random.uniform(scale_key, (D,), jnp.float32, -1.15, 1.15))
    base = jax.random.normal(base_key, (SECTIONS, ROWS, D), jnp.float32)
    base = jnp.clip(base, -4.0, 4.0)
    return (base * spread * 0.4).astype(jnp.bfloat16)


def draw_grad_log(key, part):
    key = jax.random.fold_in(key, 23)
    base_key, scale_key = jax.random.split(key, 2)
    row = jnp.arange(ROWS, dtype=jnp.float32) / ROWS
    spread = jnp.exp(jnp.log(3.0) * row[None, :, None] + jax.random.uniform(scale_key, (SECTIONS, ROWS, 1), jnp.float32, -1.15, 1.15))
    base = jax.random.normal(base_key, (SECTIONS, ROWS, D), jnp.float32)
    base = jnp.clip(base, -4.0, 4.0)
    return (base * spread * 0.4).astype(jnp.bfloat16)


def block_levels(rng, extent, pieces, smallest, top_value):
    loudness = 1.0
    for dim, shards_of in pieces:
        draws = jax.random.uniform(jax.random.fold_in(jax.random.fold_in(rng, 6), dim), (shards_of,), jnp.float32, smallest / len(pieces), top_value / len(pieces))
        loudness = loudness * jnp.repeat(jnp.exp(draws), extent[dim] // shards_of).reshape((-1,) + (1,) * (len(extent) - 1 - dim))
    return loudness


def split_up(count, total, most, slope):
    loads = [(1 << 20) // math.isqrt(standing ** slope) + 1 for standing in range(2, count + 1)]
    rest, given = total - most - (count - 1), [1] * (count - 1)
    while rest > 0:
        movable = [i for i in range(count - 1) if given[i] < most]
        whole, remaining = sum([loads[i] for i in movable]), rest
        for i in movable:
            extra = min(most - given[i], max(1, remaining * loads[i] // whole), rest)
            given[i] = given[i] + extra
            rest = rest - extra
    return np.array([most] + given)


def ragged(own_key, count, total, limit, skew):
    if count == 2:
        one = jax.random.randint(own_key, (), max(1, total - limit), min(limit, total - 1) + 1)
        return jnp.stack([one, total - one])
    tallies = jnp.asarray(split_up(count, total, limit, skew), jnp.int32)
    twos = (count - 1) // 2
    donor, receiver = tallies[1:1 + 2 * twos:2], tallies[2:2 + 2 * twos:2]
    room = jnp.minimum(donor - 1, limit - receiver)
    moved = jax.random.randint(jax.random.fold_in(own_key, 1), (twos,), 0, 1 << 20) % (room + 1)
    tallies = tallies.at[1:1 + 2 * twos:2].set(donor - moved).at[2:2 + 2 * twos:2].set(receiver + moved)
    return tallies[jax.random.permutation(jax.random.fold_in(own_key, 2), count)]


def noise(stream_key, dims, scale, bound, cuts=(), kind=jnp.bfloat16):
    entries = jax.random.normal(stream_key, dims, jnp.float32) * scale
    if len(cuts) > 0:
        entries = block_levels(stream_key, dims, cuts, -0.22, 0.18) * entries
    return jnp.clip(entries, min=-bound, max=bound).astype(kind)


def setup_inputs(seed: int = 0) -> dict:
    streams_of = jax.random.split(jax.random.key(seed), 9)
    act_log = draw_act_log(jax.random.fold_in(streams_of[8], 71), 0)
    grad_log = draw_grad_log(jax.random.fold_in(streams_of[8], 71), 0)
    failed_section = jax.random.permutation(streams_of[2], SECTIONS).astype(jnp.int32)
    live_tokens = ragged(streams_of[3], MICRO, 3 * ROWS // 4, TOK, 2).astype(jnp.int32)
    gate_weight = noise(streams_of[4], (D, FF), D ** -0.5, 0.078125, ((0, 8), (1, 64)))
    up_weight = noise(streams_of[5], (D, FF), D ** -0.5, 0.078125, ((0, 8), (1, 64)))
    down_weight = noise(streams_of[6], (FF, D), FF ** -0.5, 0.0546875, ((0, 64), (1, 8)))
    norm_gain = jnp.clip(1.0 + 0.18 * jax.random.normal(streams_of[7], (D,), jnp.float32), 0.099609375, 1.8984375).astype(jnp.bfloat16)
    return {"act_log": act_log, "grad_log": grad_log, "failed_section": failed_section, "live_tokens": live_tokens, "gate_weight": gate_weight, "up_weight": up_weight, "down_weight": down_weight, "norm_gain": norm_gain}


def split_sum(left, right):
    width = left.shape[1] // N_TENSOR
    total = jnp.zeros((left.shape[0], right.shape[1]), jnp.float32)
    for group in range(N_TENSOR):
        partial_dot = jnp.dot(left[:, group * width:(group + 1) * width], right[group * width:(group + 1) * width], preferred_element_type=jnp.float32)
        rounded = lax.optimization_barrier(partial_dot.astype(jnp.bfloat16))
        total = total + rounded.astype(jnp.float32)
    return total

def reference(act_log, grad_log, failed_section, live_tokens, gate_weight, up_weight, down_weight, norm_gain):
    failed = failed_section[0]
    source = (failed + SECTIONS - 1) % SECTIONS
    target = (failed + 1) % SECTIONS
    inputs = lax.dynamic_index_in_dim(act_log, source, 0, keepdims=False)
    logged = lax.dynamic_index_in_dim(grad_log, target, 0, keepdims=False)
    position = jnp.arange(ROWS, dtype=jnp.int32)
    limits = jnp.repeat(live_tokens, TOK, total_repeat_length=ROWS)
    keep_row = position % TOK < limits
    upstream = jnp.where(keep_row[:, None], logged, jnp.zeros_like(logged))
    inputs_wide = inputs.astype(jnp.float32)
    inv_rms = lax.rsqrt(lax.optimization_barrier(jnp.mean(inputs_wide * inputs_wide, axis=1)) + 1e-05)
    gain_wide = norm_gain.astype(jnp.float32)
    normed = (inputs_wide * inv_rms[:, None] * gain_wide).astype(jnp.bfloat16)
    gate_proj = split_sum(normed, gate_weight)
    up_proj = split_sum(normed, up_weight)
    logistic = jax.nn.sigmoid(gate_proj)
    swished = gate_proj * logistic
    slopes = logistic * (1.0 + gate_proj * (1.0 - logistic))
    hidden = (swished * up_proj).astype(jnp.bfloat16)
    hidden_grad = split_sum(upstream, down_weight.T)
    d_gate = (hidden_grad * up_proj * slopes).astype(jnp.bfloat16)
    d_up = (hidden_grad * swished).astype(jnp.bfloat16)
    grad_down = jnp.dot(hidden.T, upstream, preferred_element_type=jnp.float32).astype(jnp.bfloat16)
    grad_gate = jnp.dot(normed.T, d_gate, preferred_element_type=jnp.float32).astype(jnp.bfloat16)
    grad_up = jnp.dot(normed.T, d_up, preferred_element_type=jnp.float32).astype(jnp.bfloat16)
    d_normed = jnp.dot(d_gate, gate_weight.T, preferred_element_type=jnp.float32) + jnp.dot(d_up, up_weight.T, preferred_element_type=jnp.float32)
    grad_gain = lax.optimization_barrier(jnp.sum(d_normed * inputs_wide * inv_rms[:, None], axis=0))
    weighted = d_normed * gain_wide
    inner_sum = lax.optimization_barrier(jnp.sum(inputs_wide * weighted, axis=1))
    d_input = upstream.astype(jnp.float32) + inv_rms[:, None] * weighted - inputs_wide * (inv_rms ** 3 * inner_sum / D)[:, None]
    return (d_input.astype(jnp.bfloat16), grad_gate, grad_up, grad_down, grad_gain)
```

```python
import jax
import jax.numpy as jnp
from jax import lax
from jax.sharding import Mesh, PartitionSpec as P

AXES = ("y", "zh", "x", "zl", "c")
ROWS_AXES = ("y", "zh", "x")
F32 = jnp.float32
BF16 = jnp.bfloat16


def contract(left, right, l, r):
    return lax.dot_general(left, right, (((l,), (r,)), ((), ())), preferred_element_type=F32)


def hi_lo(v):
    hi = lax.reduce_precision(v, 8, 7)
    return hi, v - hi


def per_device(
    act_log, grad_log, failed_section, live_tokens, gate_weight, up_weight, down_weight, norm_gain
):
    ny, nzh, nx = (lax.axis_size(a) for a in ROWS_AXES)
    nzl, nc = lax.axis_size("zl"), lax.axis_size("c")
    sections = ny * nzh
    shards = sections * nx
    tokens, width = act_log.shape[1:]
    batches = live_tokens.shape[0]
    rows = batches * tokens
    live = 3 * rows // 4
    per = tokens // shards
    cycles = live // tokens
    features = width * nzl * nc
    hid = gate_weight.shape[1]
    failed = failed_section[0]
    source = (failed + sections - 1) % sections
    target = (failed + 1) % sections
    ends = jnp.cumsum(live_tokens)
    offs = ends - live_tokens

    own_off = lax.dynamic_index_in_dim(offs, lax.axis_index("x"), 0, keepdims=False) % tokens
    both = jnp.concatenate([act_log, grad_log], axis=0)
    both = jnp.concatenate([both, both], axis=1)
    rolled = lax.dynamic_slice_in_dim(both, (tokens - own_off) % tokens, tokens, 1)
    send = rolled.reshape(2, shards, per, width).swapaxes(0, 1).reshape(shards * 2 * per, width)
    recv = lax.all_to_all(send, ROWS_AXES, 0, 0, tiled=True).reshape(shards, 2, per, width)
    me = lax.axis_index(ROWS_AXES)
    got = jnp.stack(
        [
            lax.dynamic_slice_in_dim(recv[:, 0], source * nx, nx, 0),
            lax.dynamic_slice_in_dim(recv[:, 1], target * nx, nx, 0),
        ]
    )
    place = me * per + jnp.arange(per, dtype=jnp.int32)
    slot = (place[None, :] - offs[:, None]) % tokens
    cycle = (offs[:, None] + slot) // tokens
    hit = (slot < live_tokens[:, None])[:, None, :] & (
        cycle[:, None, :] == jnp.arange(cycles, dtype=jnp.int32)[None, :, None]
    )
    packed = jnp.sum(
        jnp.where(hit[None, :, :, :, None], got[:, :, None].astype(F32), 0.0), axis=1
    ).astype(BF16)
    block = cycles * per
    packed = packed.reshape(2 * block, width)

    copies = jnp.broadcast_to(packed[None], (shards,) + packed.shape).reshape(-1, width)
    whole = lax.all_to_all(copies, ROWS_AXES, 0, 0, tiled=True).reshape(shards, 2, block, width)
    inputs = whole[:, 0].reshape(live, width)
    upstream = whole[:, 1].reshape(live, width)

    inputs_wide = inputs.astype(F32)
    gain_wide = norm_gain.astype(F32)
    squares = jnp.sum(inputs_wide * inputs_wide, axis=1, keepdims=True)
    scaled = (inputs_wide * gain_wide).astype(BF16)
    sq_hi, sq_lo = hi_lo(squares)
    lanes = -(-(3 * hid + 4) // 128) * 128
    terms = jnp.concatenate(
        [
            contract(scaled, gate_weight, 1, 0).astype(BF16),
            contract(scaled, up_weight, 1, 0).astype(BF16),
            contract(upstream, down_weight, 1, 1).astype(BF16),
            sq_hi.astype(BF16),
            sq_lo.astype(BF16),
            jnp.zeros((live, lanes - 3 * hid - 2), BF16),
        ],
        axis=1,
    )
    halves = lax.all_to_all(terms, "c", 0, 0, tiled=True).reshape(nc, live // nc, lanes)
    half = jnp.sum(halves.astype(F32), axis=0).astype(BF16)
    own = live // (nc * nzl)
    quarters = lax.all_to_all(half, "zl", 0, 0, tiled=True).reshape(nzl, own, lanes)
    total = jnp.sum(quarters.astype(F32), axis=0)
    inv_rms = lax.rsqrt(
        (total[:, 3 * hid : 3 * hid + 1] + total[:, 3 * hid + 1 : 3 * hid + 2]) / features + 1e-05
    )
    gate_proj = total[:, :hid] * inv_rms
    up_proj = total[:, hid : 2 * hid] * inv_rms
    hidden_grad = total[:, 2 * hid : 3 * hid]
    logistic = jax.nn.sigmoid(gate_proj)
    swished = gate_proj * logistic
    slopes = logistic * (1.0 + gate_proj * (1.0 - logistic))
    hidden = (swished * up_proj).astype(BF16)
    d_gate = (hidden_grad * up_proj * slopes).astype(BF16)
    d_up = (hidden_grad * swished).astype(BF16)
    inner = jnp.sum(
        d_gate.astype(F32) * gate_proj + d_up.astype(F32) * up_proj, axis=1, keepdims=True
    )
    inv_hi, inv_lo = hi_lo(inv_rms)
    in_hi, in_lo = hi_lo(inner)
    mine = jnp.concatenate(
        [hidden, d_gate, d_up]
        + [v.astype(BF16) for v in (inv_hi, inv_lo, in_hi, in_lo)]
        + [jnp.zeros((own, lanes - 3 * hid - 4), BF16)],
        axis=1,
    )
    every = lax.all_gather(mine, ("c", "zl"), axis=0, tiled=True)
    hidden, d_gate, d_up = (every[:, i * hid : (i + 1) * hid] for i in range(3))
    tail = every[:, 3 * hid : 3 * hid + 4].astype(F32)
    inv_rms = tail[:, 0:1] + tail[:, 1:2]
    inner = tail[:, 2:3] + tail[:, 3:4]

    unit = inputs_wide * inv_rms
    normed = (unit * gain_wide).astype(BF16)
    d_normed = contract(d_gate, gate_weight, 1, 1) + contract(d_up, up_weight, 1, 1)
    gain_term = jnp.sum(d_normed * unit, axis=0, keepdims=True)
    term = (inv_rms * (gain_wide * d_normed - unit * (inner / features))).astype(BF16)

    own_rows = rows // shards
    shape = (nx, sections, own_rows)
    spread_row = (
        (lax.broadcasted_iota(jnp.int32, shape, 1) * nx + lax.broadcasted_iota(jnp.int32, shape, 0))
        * own_rows
        + lax.broadcasted_iota(jnp.int32, shape, 2)
    ).reshape(rows)

    def where_packed(row):
        batch = row // tokens
        pick = batch[:, None] == jnp.arange(batches, dtype=jnp.int32)[None, :]
        off = jnp.sum(jnp.where(pick, offs[None, :], 0), axis=1)
        limit = jnp.sum(jnp.where(pick, live_tokens[None, :], 0), axis=1)
        at = off + row % tokens
        index = (at % tokens) // per * block + at // tokens * per + at % per
        index = jnp.where(row % tokens < limit, index, -1)
        return (index[:, None] == jnp.arange(live, dtype=jnp.int32)[None, :]).astype(BF16)

    spread = contract(where_packed(spread_row), term, 1, 0).astype(BF16)
    gain_rows = [v.astype(BF16) for v in hi_lo(gain_term)] + [jnp.zeros((6, width), BF16)]
    gain_rows = jnp.concatenate(gain_rows, axis=0)
    out = jnp.concatenate(
        [
            spread.reshape(nx, rows // nx, width),
            jnp.broadcast_to(gain_rows[None], (nx, 8, width)),
        ],
        axis=1,
    )
    out = lax.all_to_all(out, "x", 0, 0, tiled=True)
    out = jnp.sum(out.astype(F32), axis=0)
    gain_rows = [v.astype(BF16) for v in hi_lo(out[rows // nx : rows // nx + 1] + out[rows // nx + 1 : rows // nx + 2])]
    gain_rows = jnp.concatenate(gain_rows + [jnp.zeros((6, width), BF16)], axis=0)
    out = jnp.concatenate(
        [
            out[: rows // nx].astype(BF16).reshape(sections, own_rows, width),
            jnp.broadcast_to(gain_rows[None], (sections, 8, width)),
        ],
        axis=1,
    )
    out = lax.all_to_all(out, ("y", "zh"), 0, 0, tiled=True)
    out = jnp.sum(out.astype(F32), axis=0)
    grad_gain = out[own_rows] + out[own_rows + 1]
    own_q = me * own_rows + jnp.arange(own_rows, dtype=jnp.int32)
    d_input = (contract(where_packed(own_q), upstream, 1, 0) + out[:own_rows]).astype(BF16)

    grad_down = contract(hidden, upstream, 0, 0).astype(BF16)
    grad_gate = contract(normed, d_gate, 0, 0).astype(BF16)
    grad_up = contract(normed, d_up, 0, 0).astype(BF16)
    return (d_input, grad_gate, grad_up, grad_down, grad_gain)


def solution(mesh):
    fine = Mesh(mesh.devices.reshape(8, 2, 4, 4, 2), AXES)
    section, replica, tensor = ("y", "zh"), "x", ("zl", "c")
    split = ("y", "zh", "x")
    in_specs = (
        P(section, replica, tensor),
        P(section, replica, tensor),
        P(),
        P(),
        P(tensor, split),
        P(tensor, split),
        P(split, tensor),
        P(tensor),
    )
    out_specs = (
        P(split, tensor),
        P(tensor, split),
        P(tensor, split),
        P(split, tensor),
        P(tensor),
    )
    return jax.shard_map(
        per_device, mesh=fine, in_specs=in_specs, out_specs=out_specs, check_vma=False
    )
```

```python
import functools

import jax
import jax.numpy as jnp
from jax import lax
from jax.experimental import pallas as pl
from jax.experimental.pallas import tpu as pltpu
from jax.sharding import Mesh, PartitionSpec as P

AXES = ("y", "zh", "x", "zl", "c")
ROWS_AXES = ("y", "zh", "x")
F32 = jnp.float32
BF16 = jnp.bfloat16
WIDE = 256
VMEM = pl.BlockSpec(memory_space=pltpu.VMEM)
SMEM = pl.BlockSpec(memory_space=pltpu.SMEM)


def contract(left, right, l, r):
    return lax.dot_general(left, right, (((l,), (r,)), ((), ())), preferred_element_type=F32)


def hi_lo(v):
    hi = lax.reduce_precision(v, 8, 7)
    return hi, v - hi


def call(body, outs, scratch, flops, *args):
    moved = sum(a.size * a.dtype.itemsize for a in args) + sum(
        o.size * o.dtype.itemsize for o in jax.tree.leaves(outs)
    )
    return pl.pallas_call(
        body,
        out_shape=outs,
        in_specs=[SMEM if a.ndim == 1 else VMEM for a in args],
        out_specs=jax.tree.map(lambda _: VMEM, outs),
        scratch_shapes=scratch,
        compiler_params=pltpu.CompilerParams(vmem_limit_bytes=48 * 1024 * 1024),
        cost_estimate=pl.CostEstimate(flops=flops, bytes_accessed=moved, transcendentals=0),
    )(*args)


def pick(refs, k):
    own, right, left, over_in, over_up = refs
    if k < 3:
        ref = (own, right, left)[k]
        return ref[0], ref[1]
    return over_in[...], over_up[...]


def terms_kernel(hid, c_ref, own, right, left, over_in, over_up, gain, gate, up, down, keep, send):
    core = c_ref[0]
    gain_wide = gain[...].astype(F32)
    for k in range(4):
        inputs, upstream = pick((own, right, left, over_in, over_up), k)
        n = inputs.shape[0]
        wide = inputs.astype(F32)
        squares = jnp.sum(wide * wide, axis=1, keepdims=True)
        sq_hi = squares.astype(BF16).astype(F32)
        scaled = (wide * gain_wide).astype(BF16)
        lane = lax.broadcasted_iota(jnp.int32, (n, WIDE), 1)
        first = contract(scaled, gate[...], 1, 0)
        first = jnp.where(lane == hid, sq_hi, jnp.where(lane == hid + 1, squares - sq_hi, first))
        parts = (
            first.astype(BF16),
            contract(scaled, up[...], 1, 0).astype(BF16),
            contract(upstream, down[...], 1, 1).astype(BF16),
        )
        at = (k % 2) * n

        def store(out):
            for i, part in enumerate(parts):
                out[at : at + n, i * WIDE : (i + 1) * WIDE] = part

        pl.when(core == k // 2)(functools.partial(store, keep))
        pl.when(core != k // 2)(functools.partial(store, send))


def pair_kernel(keep, recv, out):
    out[...] = (keep[...].astype(F32) + recv[...].astype(F32)).astype(BF16)


def point_kernel(hid, features, quarters, out):
    def total(i):
        s = slice(i * WIDE, (i + 1) * WIDE)
        return sum(quarters[z, :, s].astype(F32) for z in range(1, 4)) + quarters[0, :, s].astype(F32)

    gate, up, hidden_grad = total(0), total(1), total(2)
    lane = lax.broadcasted_iota(jnp.int32, gate.shape, 1)
    squares = jnp.sum(jnp.where((lane == hid) | (lane == hid + 1), gate, 0.0), axis=1, keepdims=True)
    inv_rms = lax.rsqrt(squares / features + 1e-05)
    gate = jnp.where(lane < hid, gate, 0.0) * inv_rms
    up = up * inv_rms
    logistic = jax.nn.sigmoid(gate)
    swished = gate * logistic
    slopes = logistic * (1.0 + gate * (1.0 - logistic))
    hidden = swished * up
    d_gate = (hidden_grad * up * slopes).astype(BF16)
    d_up = (hidden_grad * swished).astype(BF16)
    inner = jnp.sum(d_gate.astype(F32) * gate + d_up.astype(F32) * up, axis=1, keepdims=True)
    for i, v in enumerate((inv_rms, inner)):
        hi = v.astype(BF16).astype(F32)
        hidden = jnp.where(lane == hid + 2 * i, hi, jnp.where(lane == hid + 2 * i + 1, v - hi, hidden))
    out[:, :WIDE] = hidden.astype(BF16)
    out[:, WIDE : 2 * WIDE] = d_gate
    out[:, 2 * WIDE :] = d_up


def tails(hid, pay):
    head = pay[:, :WIDE].astype(F32)
    lane = lax.broadcasted_iota(jnp.int32, head.shape, 1)

    def two(i):
        return jnp.sum(
            jnp.where((lane == hid + i) | (lane == hid + i + 1), head, 0.0), axis=1, keepdims=True
        )

    return two(0), two(2)


def term_kernel(
    hid, features, c_ref, own, right, left, over_in, over_up, mine, theirs, gain, gate, up,
    index, index_own, out, up_own, pay_ref, term_ref,
):
    core = c_ref[0]
    pay_ref[core] = mine[...]
    pay_ref[1 - core] = theirs[...]
    gain_wide = gain[...].astype(F32)
    gain_term = jnp.zeros(gain_wide.shape, F32)
    own_total = jnp.zeros(up_own.shape, F32)
    for k in range(4):
        inputs, upstream = pick((own, right, left, over_in, over_up), k)
        n = inputs.shape[0]
        at = (k % 2) * n
        pay = pay_ref[k // 2, at : at + n, :]
        inv_rms, inner = tails(hid, pay)
        d_normed = contract(pay[:, WIDE : 2 * WIDE], gate[...], 1, 1) + contract(
            pay[:, 2 * WIDE :], up[...], 1, 1
        )
        unit = inputs.astype(F32) * inv_rms
        gain_term = gain_term + jnp.sum(d_normed * unit, axis=0, keepdims=True)
        term = inv_rms * (gain_wide * d_normed - unit * (inner / features))
        term_ref[k * n : (k + 1) * n, :] = term.astype(BF16)
        column = lax.broadcasted_iota(jnp.int32, (up_own.shape[0], n), 1) + k * n
        hot = jnp.where(index_own[...] == column, 1.0, 0.0).astype(BF16)
        own_total = own_total + contract(hot, upstream, 1, 0)
    up_own[...] = own_total.astype(BF16)
    gain_hi = gain_term.astype(BF16).astype(F32)
    rows = index.shape[0] // 4
    extra = out.shape[1] - rows
    row = lax.broadcasted_iota(jnp.int32, (extra, gain_term.shape[1]), 0)
    extras = jnp.where(row == 0, gain_hi, jnp.where(row == 1, gain_term - gain_hi, 0.0)).astype(BF16)
    live = term_ref.shape[0]
    column = lax.broadcasted_iota(jnp.int32, (rows, live), 1)
    for q in range(4):
        hot = jnp.where(index[q * rows : (q + 1) * rows, :] == column, 1.0, 0.0).astype(BF16)
        out[q, :rows, :] = contract(hot, term_ref[...], 1, 0).astype(BF16)
        out[q, rows:, :] = extras


def grads_kernel(
    hid, c_ref, own, right, left, over_in, over_up, mine, theirs, gain,
    grad_gate, grad_up, grad_down, pay_ref, normed_ref, up_ref,
):
    core = c_ref[0]
    half = mine.shape[0]
    first = pl.multiple_of(core * half, half)
    second = pl.multiple_of((1 - core) * half, half)
    pay_ref[pl.ds(first, half), :] = mine[...]
    pay_ref[pl.ds(second, half), :] = theirs[...]
    gain_wide = gain[...].astype(F32)
    for k in range(4):
        inputs, upstream = pick((own, right, left, over_in, over_up), k)
        n = inputs.shape[0]
        inv_rms, _ = tails(hid, pay_ref[k * n : (k + 1) * n, :])
        normed_ref[k * n : (k + 1) * n, :] = (inputs.astype(F32) * inv_rms * gain_wide).astype(BF16)
        up_ref[k * n : (k + 1) * n, :] = upstream
    hidden = pay_ref[:, :WIDE]
    grad_down[...] = contract(hidden, up_ref[...], 0, 0)[:hid].astype(BF16)
    normed = normed_ref[...]
    grad_gate[...] = contract(normed, pay_ref[:, WIDE : 2 * WIDE], 0, 0)[:, :hid].astype(BF16)
    grad_up[...] = contract(normed, pay_ref[:, 2 * WIDE :], 0, 0)[:, :hid].astype(BF16)


def per_device(
    act_log, grad_log, failed_section, live_tokens, gate_weight, up_weight, down_weight, norm_gain
):
    ny, nzh, nx = (lax.axis_size(a) for a in ROWS_AXES)
    nzl, nc = lax.axis_size("zl"), lax.axis_size("c")
    sections = ny * nzh
    shards = sections * nx
    tokens, width = act_log.shape[1:]
    batches = live_tokens.shape[0]
    rows = batches * tokens
    live = 3 * rows // 4
    per = tokens // shards
    cycles = live // tokens
    features = float(width * nzl * nc)
    hid = gate_weight.shape[1]
    failed = failed_section[0]
    source = (failed + sections - 1) % sections
    target = (failed + 1) % sections
    batch = jnp.arange(batches, dtype=jnp.int32)
    offs = jnp.sum(jnp.where(batch[None, :] < batch[:, None], live_tokens[None, :], 0), axis=1)
    x = lax.axis_index("x")
    core = lax.axis_index("c").astype(jnp.int32).reshape(1)
    me = lax.axis_index(ROWS_AXES)

    own_off = jnp.sum(jnp.where(batch < x, live_tokens, 0))
    out_row = lax.broadcasted_iota(jnp.int32, (2 * tokens, tokens), 0)
    from_row = lax.broadcasted_iota(jnp.int32, (2 * tokens, tokens), 1)
    slot = (out_row // (2 * per) * per + out_row % per - own_off) % tokens
    hot = slot == from_row
    is_up = out_row % (2 * per) >= per
    send = (
        contract((hot & ~is_up).astype(BF16), act_log[0], 1, 0)
        + contract((hot & is_up).astype(BF16), grad_log[0], 1, 0)
    ).astype(BF16)
    recv = lax.all_to_all(send, ROWS_AXES, 0, 0, tiled=True).reshape(shards, 2 * per, width)
    got = jnp.stack(
        [
            lax.dynamic_slice_in_dim(recv, source * nx, nx, 0)[:, :per],
            lax.dynamic_slice_in_dim(recv, target * nx, nx, 0)[:, per:],
        ]
    )
    place = me * per + jnp.arange(per, dtype=jnp.int32)
    slot = (place[None, :] - offs[:, None]) % tokens
    cycle = (offs[:, None] + slot) // tokens
    hit = (slot < live_tokens[:, None])[:, None, :] & (
        cycle[:, None, :] == jnp.arange(cycles, dtype=jnp.int32)[None, :, None]
    )
    packed = jnp.sum(
        jnp.where(hit[None, :, :, :, None], got[:, :, None].astype(F32), 0.0), axis=1
    ).astype(BF16)
    block = cycles * per
    packed = packed.reshape(2 * block, width)

    copies = jnp.broadcast_to(packed[None], (sections,) + packed.shape).reshape(-1, width)
    column = lax.all_to_all(copies, ("y", "zh"), 0, 0, tiled=True)
    part = sections * block
    out_row = lax.broadcasted_iota(jnp.int32, (2 * part, 2 * part), 0)
    from_row = lax.broadcasted_iota(jnp.int32, (2 * part, 2 * part), 1)
    at = out_row % part
    hot = (at // block * 2 + out_row // part) * block + at % block == from_row
    own = contract(hot.astype(BF16), column, 1, 0).astype(BF16).reshape(2, part, width)
    ahead = [(i, (i + 1) % nx) for i in range(nx)]
    back = [(i, (i - 1) % nx) for i in range(nx)]
    right = lax.ppermute(own, "x", ahead)
    left = lax.ppermute(own, "x", back)
    over_in = lax.ppermute(right[0], "x", ahead)
    over_up = lax.ppermute(left[1], "x", back)
    blocks = (own, right, left, over_in, over_up)

    pad = ((0, 0), (0, WIDE - hid))
    gate_pad, up_pad = jnp.pad(gate_weight, pad), jnp.pad(up_weight, pad)
    down_pad = jnp.pad(down_weight, pad[::-1])
    gain = norm_gain.reshape(1, width)
    lanes = 3 * WIDE
    half = live // nc
    own_count = half // nzl

    def shape(*dims, dtype=BF16):
        return jax.ShapeDtypeStruct(dims, dtype)

    product = 2 * live * width * WIDE
    keep, give = call(
        functools.partial(terms_kernel, hid), (shape(half, lanes), shape(half, lanes)), [], 3 * product,
        core, *blocks, gain, gate_pad, up_pad, down_pad,
    )
    taken = lax.ppermute(give, "c", [(0, 1), (1, 0)])
    pair = call(pair_kernel, shape(half, lanes), [], half * lanes, keep, taken)
    quarters = lax.all_to_all(pair, "zl", 0, 0, tiled=True).reshape(nzl, own_count, lanes)
    point = call(
        functools.partial(point_kernel, hid, features), shape(own_count, lanes), [],
        20 * own_count * lanes, quarters,
    )
    mine = lax.all_gather(point, "zl", axis=0, tiled=True)
    theirs = lax.ppermute(mine, "c", [(0, 1), (1, 0)])

    own_rows = rows // shards

    def where_packed(row):
        at_batch = row // tokens
        chosen = at_batch[:, None] == batch[None, :]
        off = jnp.sum(jnp.where(chosen, offs[None, :], 0), axis=1)
        limit = jnp.sum(jnp.where(chosen, live_tokens[None, :], 0), axis=1)
        at = off + row % tokens
        device = at % tokens // per
        turn = (device - x) % nx
        held = jnp.where(turn == nx - 1, 1, jnp.where(turn == 1, 2, jnp.where(turn == 2, 3, 0)))
        index = held * part + device // nx * block + at // tokens * per + at % per
        return jnp.where(row % tokens < limit, index, -1)[:, None]

    dims = (nx, sections, own_rows)
    spread_row = (
        (lax.broadcasted_iota(jnp.int32, dims, 1) * nx + lax.broadcasted_iota(jnp.int32, dims, 0))
        * own_rows
        + lax.broadcasted_iota(jnp.int32, dims, 2)
    ).reshape(rows)
    index = where_packed(spread_row)
    index_own = where_packed(me * own_rows + jnp.arange(own_rows, dtype=jnp.int32))
    count = rows // nx
    out, up_own = call(
        functools.partial(term_kernel, hid, features),
        (shape(nx, count + 16, width), shape(own_rows, width)),
        [pltpu.VMEM((nc, half, lanes), BF16), pltpu.VMEM((live, width), BF16)],
        5 * product,
        core, *blocks, mine, theirs, gain, gate_pad, up_pad, index, index_own,
    )
    out = lax.all_to_all(out, "x", 0, 0, tiled=True)
    out = jnp.sum(out.astype(F32), axis=0)
    gain_rows = [v.astype(BF16) for v in hi_lo(out[count : count + 1] + out[count + 1 : count + 2])]
    gain_rows = jnp.concatenate(gain_rows + [jnp.zeros((6, width), BF16)], axis=0)
    out = jnp.concatenate(
        [
            out[:count].astype(BF16).reshape(sections, own_rows, width),
            jnp.broadcast_to(gain_rows[None], (sections, 8, width)),
        ],
        axis=1,
    )
    out = lax.all_to_all(out, ("y", "zh"), 0, 0, tiled=True)
    out = jnp.sum(out.astype(F32), axis=0)
    grad_gain = out[own_rows] + out[own_rows + 1]
    d_input = (up_own.astype(F32) + out[:own_rows]).astype(BF16)

    grad_gate, grad_up, grad_down = call(
        functools.partial(grads_kernel, hid),
        (shape(width, hid), shape(width, hid), shape(hid, width)),
        [
            pltpu.VMEM((live, lanes), BF16),
            pltpu.VMEM((live, width), BF16),
            pltpu.VMEM((live, width), BF16),
        ],
        3 * product,
        core, *blocks, mine, theirs, gain,
    )
    return (d_input, grad_gate, grad_up, grad_down, grad_gain)


def solution(mesh):
    fine = Mesh(mesh.devices.reshape(8, 2, 4, 4, 2), AXES)
    section, replica, tensor = ("y", "zh"), "x", ("zl", "c")
    split = ("y", "zh", "x")
    in_specs = (
        P(section, replica, tensor),
        P(section, replica, tensor),
        P(),
        P(),
        P(tensor, split),
        P(tensor, split),
        P(split, tensor),
        P(tensor),
    )
    out_specs = (
        P(split, tensor),
        P(tensor, split),
        P(tensor, split),
        P(split, tensor),
        P(tensor),
    )
    return jax.shard_map(
        per_device, mesh=fine, in_specs=in_specs, out_specs=out_specs, check_vma=False
    )
```

```python
import functools

import jax
import jax.numpy as jnp
from jax import lax
from jax.experimental import pallas as pl
from jax.experimental.pallas import tpu as pltpu
from jax.sharding import Mesh, PartitionSpec as P

AXES = ("y", "zh", "x", "zl", "c")
ROWS_AXES = ("y", "zh", "x")
F32 = jnp.float32
BF16 = jnp.bfloat16
WIDE = 256
VMEM = pl.BlockSpec(memory_space=pltpu.VMEM)
SMEM = pl.BlockSpec(memory_space=pltpu.SMEM)


def contract(left, right, l, r):
    return lax.dot_general(left, right, (((l,), (r,)), ((), ())), preferred_element_type=F32)


def hi_lo(v):
    hi = lax.reduce_precision(v, 8, 7)
    return hi, v - hi


def call(body, outs, scratch, flops, *args):
    moved = sum(a.size * a.dtype.itemsize for a in args) + sum(
        o.size * o.dtype.itemsize for o in jax.tree.leaves(outs)
    )
    return pl.pallas_call(
        body,
        out_shape=outs,
        in_specs=[SMEM if a.ndim == 1 else VMEM for a in args],
        out_specs=jax.tree.map(lambda _: VMEM, outs),
        scratch_shapes=scratch,
        compiler_params=pltpu.CompilerParams(vmem_limit_bytes=48 * 1024 * 1024),
        cost_estimate=pl.CostEstimate(flops=flops, bytes_accessed=moved, transcendentals=0),
    )(*args)


def pick(refs, k):
    own, right, left, over_in, over_up = refs
    if k < 3:
        ref = (own, right, left)[k]
        return ref[0], ref[1]
    return over_in[...], over_up[...]


def log2(n):
    assert n & (n - 1) == 0
    return n.bit_length() - 1


CORE, REPLICA, ME, OWN_OFF, LINE, LIVE = 0, 1, 2, 3, 4, 5


def scatter_kernel(per, nums, act, grad, send):
    tokens = act.shape[1]
    shape = (2 * tokens, tokens)
    row = lax.broadcasted_iota(jnp.int32, shape, 0)
    column = lax.broadcasted_iota(jnp.int32, shape, 1)
    place = (row >> log2(2 * per) << log2(per)) + (row & (per - 1))
    hot = ((place - nums[OWN_OFF] + tokens) & (tokens - 1)) == column
    is_up = (row & per) != 0
    first = jnp.where(hot & ~is_up, 1.0, 0.0).astype(BF16)
    second = jnp.where(hot & is_up, 1.0, 0.0).astype(BF16)
    send[...] = (contract(first, act[0], 1, 0) + contract(second, grad[0], 1, 0)).astype(BF16)


def terms_kernel(hid, nums, own, right, left, over_in, over_up, gain, gate, up, down, keep, send):
    core = nums[CORE]
    gain_wide = gain[...].astype(F32)
    for k in range(4):
        inputs, upstream = pick((own, right, left, over_in, over_up), k)
        n = inputs.shape[0]
        wide = inputs.astype(F32)
        squares = jnp.sum(wide * wide, axis=1, keepdims=True)
        sq_hi = squares.astype(BF16).astype(F32)
        scaled = (wide * gain_wide).astype(BF16)
        lane = lax.broadcasted_iota(jnp.int32, (n, WIDE), 1)
        first = contract(scaled, gate[...], 1, 1)
        first = jnp.where(lane == hid, sq_hi, jnp.where(lane == hid + 1, squares - sq_hi, first))
        parts = (
            first.astype(BF16),
            contract(scaled, up[...], 1, 1).astype(BF16),
            contract(upstream, down[...], 1, 1).astype(BF16),
        )
        at = (k % 2) * n

        def store(out):
            for i, part in enumerate(parts):
                out[at : at + n, i * WIDE : (i + 1) * WIDE] = part

        pl.when(core == k // 2)(functools.partial(store, keep))
        pl.when(core != k // 2)(functools.partial(store, send))


def pair_kernel(nums, keep, recv, *outs):
    own = outs[0].shape[0]
    for i, out in enumerate(outs):
        chunk = (nums[LINE] + i) & (len(outs) - 1)
        rows = pl.ds(pl.multiple_of(chunk * own, own), own)
        out[...] = (keep[rows, :].astype(F32) + recv[rows, :].astype(F32)).astype(BF16)


def point_kernel(hid, features, *refs):
    terms, out = refs[:-1], refs[-1]

    def total(i):
        s = slice(i * WIDE, (i + 1) * WIDE)
        return sum((t[:, s].astype(F32) for t in terms[1:]), terms[0][:, s].astype(F32))

    gate, up, hidden_grad = total(0), total(1), total(2)
    lane = lax.broadcasted_iota(jnp.int32, gate.shape, 1)
    squares = jnp.sum(jnp.where((lane == hid) | (lane == hid + 1), gate, 0.0), axis=1, keepdims=True)
    inv_rms = lax.rsqrt(squares / features + 1e-05)
    gate = jnp.where(lane < hid, gate, 0.0) * inv_rms
    up = up * inv_rms
    logistic = jax.nn.sigmoid(gate)
    swished = gate * logistic
    slopes = logistic * (1.0 + gate * (1.0 - logistic))
    hidden = swished * up
    d_gate = (hidden_grad * up * slopes).astype(BF16)
    d_up = (hidden_grad * swished).astype(BF16)
    inner = jnp.sum(d_gate.astype(F32) * gate + d_up.astype(F32) * up, axis=1, keepdims=True)
    lane = lax.broadcasted_iota(jnp.int32, (gate.shape[0], 4), 1)
    inv_hi = inv_rms.astype(BF16).astype(F32)
    in_hi = inner.astype(BF16).astype(F32)
    tail = jnp.where(
        lane == 0, inv_hi, jnp.where(lane == 1, inv_rms - inv_hi, jnp.where(lane == 2, in_hi, inner - in_hi))
    )
    out[:, :hid] = hidden[:, :hid].astype(BF16)
    out[:, hid : 2 * hid] = d_gate[:, :hid]
    out[:, 2 * hid : 3 * hid] = d_up[:, :hid]
    out[:, 3 * hid :] = tail.astype(BF16)


def rows_of(every, k, n):
    cores, own = 2, n // 2
    at = [(((k % 2) * 2 + j) * cores + k // 2) * own for j in range(2)]
    return jnp.concatenate([every[a : a + own, :] for a in at], axis=0)


def where_packed(nums, row, batches, tokens, per, nx, block, part):
    batch = row >> log2(tokens)
    slot = row & (tokens - 1)
    limit, off = jnp.zeros_like(row), jnp.zeros_like(row)
    for b in range(batches):
        limit = jnp.where(batch == b, nums[LIVE + b], limit)
        off = jnp.where(batch == b, nums[LIVE + batches + b], off)
    at = off + slot
    device = (at & (tokens - 1)) >> log2(per)
    turn = (device - nums[REPLICA] + nx) & (nx - 1)
    held = jnp.where(turn == nx - 1, 1, jnp.where(turn == 1, 2, jnp.where(turn == 2, 3, 0)))
    index = held * part + (device >> log2(nx)) * block + (at >> log2(tokens)) * per + (at & (per - 1))
    return jnp.where(slot < limit, index, -1)


def term_kernel(
    hid, features, plan, nums, own, right, left, over_in, over_up, every, gain, gate, up,
    out, up_own, term_ref,
):
    nx = out.shape[0]
    gain_wide = gain[...].astype(F32)
    gain_term = jnp.zeros(gain_wide.shape, F32)
    own_rows = up_own.shape[0]
    own_total = jnp.zeros(up_own.shape, F32)
    row = nums[ME] * own_rows + lax.broadcasted_iota(jnp.int32, (own_rows, 1), 0)
    index = where_packed(nums, row, *plan)
    for k in range(4):
        inputs, upstream = pick((own, right, left, over_in, over_up), k)
        n = inputs.shape[0]
        pay = rows_of(every, k, n)
        tail = pay[:, 3 * hid :].astype(F32)
        inv_rms = tail[:, 0:1] + tail[:, 1:2]
        inner = tail[:, 2:3] + tail[:, 3:4]
        d_normed = contract(pay[:, hid : 2 * hid], gate[...], 1, 0) + contract(
            pay[:, 2 * hid : 3 * hid], up[...], 1, 0
        )
        unit = inputs.astype(F32) * inv_rms
        gain_term = gain_term + jnp.sum(d_normed * unit, axis=0, keepdims=True)
        term = inv_rms * (gain_wide * d_normed - unit * (inner / features))
        term_ref[k * n : (k + 1) * n, :] = term.astype(BF16)
        column = lax.broadcasted_iota(jnp.int32, (own_rows, n), 1) + k * n
        hot = jnp.where(index == column, 1.0, 0.0).astype(BF16)
        own_total = own_total + contract(hot, upstream, 1, 0)
    up_own[...] = own_total.astype(BF16)
    gain_hi = gain_term.astype(BF16).astype(F32)
    rows = plan[0] * plan[1] // nx
    extra = out.shape[1] - rows
    row = lax.broadcasted_iota(jnp.int32, (extra, gain_term.shape[1]), 0)
    extras = jnp.where(row == 0, gain_hi, jnp.where(row == 1, gain_term - gain_hi, 0.0)).astype(BF16)
    live = term_ref.shape[0]
    column = lax.broadcasted_iota(jnp.int32, (rows, live), 1)
    i = lax.broadcasted_iota(jnp.int32, (rows, 1), 0)
    for q in range(nx):
        row = (((i >> log2(own_rows)) * nx + q) << log2(own_rows)) + (i & (own_rows - 1))
        hot = jnp.where(where_packed(nums, row, *plan) == column, 1.0, 0.0).astype(BF16)
        out[q, :rows, :] = contract(hot, term_ref[...], 1, 0).astype(BF16)
        out[q, rows:, :] = extras


def grads_kernel(
    hid, own, right, left, over_in, over_up, every, gain,
    grad_gate, grad_up, grad_down, pay_ref, normed_ref, up_ref,
):
    gain_wide = gain[...].astype(F32)
    for k in range(4):
        inputs, upstream = pick((own, right, left, over_in, over_up), k)
        n = inputs.shape[0]
        s = slice(k * n, (k + 1) * n)
        pay = rows_of(every, k, n)
        tail = pay[:, 3 * hid :].astype(F32)
        inv_rms = tail[:, 0:1] + tail[:, 1:2]
        for i in range(3):
            pay_ref[i, s, :hid] = pay[:, i * hid : (i + 1) * hid]
        normed_ref[s, :] = (inputs.astype(F32) * inv_rms * gain_wide).astype(BF16)
        up_ref[s, :] = upstream
    grad_down[...] = contract(pay_ref[0, :, :hid], up_ref[...], 0, 0).astype(BF16)
    normed = normed_ref[...]
    grad_gate[...] = contract(pay_ref[1, :, :hid], normed, 0, 0).astype(BF16)
    grad_up[...] = contract(pay_ref[2, :, :hid], normed, 0, 0).astype(BF16)


def per_device(
    act_log, grad_log, failed_section, live_tokens, gate_weight, up_weight, down_weight, norm_gain
):
    ny, nzh, nx = (lax.axis_size(a) for a in ROWS_AXES)
    nzl, nc = lax.axis_size("zl"), lax.axis_size("c")
    sections = ny * nzh
    shards = sections * nx
    tokens, width = act_log.shape[1:]
    batches = live_tokens.shape[0]
    rows = batches * tokens
    live = 3 * rows // 4
    per = tokens // shards
    cycles = live // tokens
    features = float(width * nzl * nc)
    hid = gate_weight.shape[1]
    failed = failed_section[0]
    source = (failed + sections - 1) % sections
    target = (failed + 1) % sections
    batch = jnp.arange(batches, dtype=jnp.int32)
    offs = jnp.sum(jnp.where(batch[None, :] < batch[:, None], live_tokens[None, :], 0), axis=1)
    x = lax.axis_index("x")
    me = lax.axis_index(ROWS_AXES)
    plan = (batches, tokens, per, nx, cycles * per, sections * cycles * per)

    def shape(*dims, dtype=BF16):
        return jax.ShapeDtypeStruct(dims, dtype)

    own_off = jnp.sum(jnp.where(batch < x, live_tokens, 0)) % tokens
    nums = jnp.stack([lax.axis_index("c"), x, me, own_off, lax.axis_index("zl")]).astype(jnp.int32)
    nums = jnp.concatenate([nums, live_tokens, offs.astype(jnp.int32)])
    send = call(
        functools.partial(scatter_kernel, per), shape(2 * tokens, width), [],
        4 * tokens * tokens * width, nums, act_log, grad_log,
    )
    recv = lax.all_to_all(send, ROWS_AXES, 0, 0, tiled=True).reshape(shards, 2 * per, width)
    got = jnp.stack(
        [
            lax.dynamic_slice_in_dim(recv, source * nx, nx, 0)[:, :per],
            lax.dynamic_slice_in_dim(recv, target * nx, nx, 0)[:, per:],
        ]
    )
    place = me * per + jnp.arange(per, dtype=jnp.int32)
    slot = (place[None, :] - offs[:, None]) % tokens
    cycle = (offs[:, None] + slot) // tokens
    hit = (slot < live_tokens[:, None])[:, None, :] & (
        cycle[:, None, :] == jnp.arange(cycles, dtype=jnp.int32)[None, :, None]
    )
    packed = jnp.sum(
        jnp.where(hit[None, :, :, :, None], got[:, :, None].astype(F32), 0.0), axis=1
    ).astype(BF16)
    block = cycles * per
    packed = packed.reshape(2 * block, width)

    copies = jnp.broadcast_to(packed[None], (sections,) + packed.shape).reshape(-1, width)
    column = lax.all_to_all(copies, ("y", "zh"), 0, 0, tiled=True)
    part = sections * block
    out_row = lax.broadcasted_iota(jnp.int32, (2 * part, 2 * part), 0)
    from_row = lax.broadcasted_iota(jnp.int32, (2 * part, 2 * part), 1)
    at = out_row % part
    hot = (at // block * 2 + out_row // part) * block + at % block == from_row
    own = contract(hot.astype(BF16), column, 1, 0).astype(BF16).reshape(2, part, width)
    ahead = [(i, (i + 1) % nx) for i in range(nx)]
    back = [(i, (i - 1) % nx) for i in range(nx)]
    right = lax.ppermute(own, "x", ahead)
    left = lax.ppermute(own, "x", back)
    over_in = lax.ppermute(right[0], "x", ahead)
    over_up = lax.ppermute(left[1], "x", back)
    blocks = (own, right, left, over_in, over_up)

    pad = ((0, WIDE - hid), (0, 0))
    gate_rows, up_rows = gate_weight.T, up_weight.T
    gate_pad, up_pad, down_pad = (jnp.pad(w, pad) for w in (gate_rows, up_rows, down_weight))
    gain = norm_gain.reshape(1, width)
    lanes = 3 * WIDE
    half = live // nc
    own_count = half // nzl

    product = 2 * live * width * WIDE
    keep, give = call(
        functools.partial(terms_kernel, hid), (shape(half, lanes), shape(half, lanes)), [], 3 * product,
        nums, *blocks, gain, gate_pad, up_pad, down_pad,
    )
    taken = lax.ppermute(give, "c", [(0, 1), (1, 0)])
    chunk = shape(own_count, lanes)
    pairs = call(pair_kernel, (chunk,) * nzl, [], half * lanes, nums, keep, taken)
    others = [
        lax.ppermute(pairs[i], "zl", [(a, (a + i) % nzl) for a in range(nzl)]) for i in range(1, nzl)
    ]
    point = call(
        functools.partial(point_kernel, hid, features), shape(own_count, 3 * hid + 4), [],
        20 * own_count * lanes, pairs[0], *others,
    )
    every = lax.all_gather(point, ("zl", "c"), axis=0, tiled=True)

    own_rows = rows // shards
    count = rows // nx
    out, up_own = call(
        functools.partial(term_kernel, hid, features, plan),
        (shape(nx, count + 16, width), shape(own_rows, width)),
        [pltpu.VMEM((live, width), BF16)],
        5 * product,
        nums, *blocks, every, gain, gate_rows, up_rows,
    )
    out = lax.all_to_all(out, "x", 0, 0, tiled=True)
    out = jnp.sum(out.astype(F32), axis=0)
    gain_rows = [v.astype(BF16) for v in hi_lo(out[count : count + 1] + out[count + 1 : count + 2])]
    gain_rows = jnp.concatenate(gain_rows + [jnp.zeros((6, width), BF16)], axis=0)
    out = jnp.concatenate(
        [
            out[:count].astype(BF16).reshape(sections, own_rows, width),
            jnp.broadcast_to(gain_rows[None], (sections, 8, width)),
        ],
        axis=1,
    )
    out = lax.all_to_all(out, ("y", "zh"), 0, 0, tiled=True)
    out = jnp.sum(out.astype(F32), axis=0)
    grad_gain = out[own_rows] + out[own_rows + 1]
    d_input = (up_own.astype(F32) + out[:own_rows]).astype(BF16)

    grad_gate, grad_up, grad_down = call(
        functools.partial(grads_kernel, hid),
        (shape(hid, width),) * 3,
        [
            pltpu.VMEM((3, live, WIDE), BF16),
            pltpu.VMEM((live, width), BF16),
            pltpu.VMEM((live, width), BF16),
        ],
        3 * product,
        *blocks, every, gain,
    )
    return (d_input, grad_gate.T, grad_up.T, grad_down, grad_gain)


def solution(mesh):
    fine = Mesh(mesh.devices.reshape(8, 2, 4, 4, 2), AXES)
    section, replica, tensor = ("y", "zh"), "x", ("zl", "c")
    split = ("y", "zh", "x")
    in_specs = (
        P(section, replica, tensor),
        P(section, replica, tensor),
        P(),
        P(),
        P(tensor, split),
        P(tensor, split),
        P(split, tensor),
        P(tensor),
    )
    out_specs = (
        P(split, tensor),
        P(tensor, split),
        P(tensor, split),
        P(split, tensor),
        P(tensor),
    )
    return jax.shard_map(
        per_device, mesh=fine, in_specs=in_specs, out_specs=out_specs, check_vma=False
    )
```

```python
import functools

import jax
import jax.numpy as jnp
from jax import lax
from jax.experimental import pallas as pl
from jax.experimental.pallas import tpu as pltpu
from jax.sharding import Mesh, PartitionSpec as P

AXES = ("y", "zh", "x", "zl", "c")
ROWS_AXES = ("y", "zh", "x")
F32 = jnp.float32
BF16 = jnp.bfloat16
WIDE = 256
VMEM = pl.BlockSpec(memory_space=pltpu.VMEM)
SMEM = pl.BlockSpec(memory_space=pltpu.SMEM)


def contract(left, right, l, r):
    return lax.dot_general(left, right, (((l,), (r,)), ((), ())), preferred_element_type=F32)


def call(body, outs, scratch, flops, *args):
    moved = sum(a.size * a.dtype.itemsize for a in args) + sum(
        o.size * o.dtype.itemsize for o in jax.tree.leaves(outs)
    )
    return pl.pallas_call(
        body,
        out_shape=outs,
        in_specs=[SMEM if a.ndim == 1 else VMEM for a in args],
        out_specs=jax.tree.map(lambda _: VMEM, outs),
        scratch_shapes=scratch,
        compiler_params=pltpu.CompilerParams(vmem_limit_bytes=48 * 1024 * 1024),
        cost_estimate=pl.CostEstimate(flops=flops, bytes_accessed=moved, transcendentals=0),
    )(*args)


def pick(refs, k):
    own, right, left, over_in, over_up = refs
    if k < 3:
        ref = (own, right, left)[k]
        return ref[0], ref[1]
    return over_in[...], over_up[...]


def log2(n):
    assert n & (n - 1) == 0
    return n.bit_length() - 1


CORE, REPLICA, ME, LINE, LIVE = 0, 1, 2, 3, 4


def scatter_kernel(per, live, act, grad, send):
    tokens = act.shape[1]
    x = lax.axis_index("x")
    off = jnp.int32(0)
    for b in range(live.shape[0] - 1):
        off = off + jnp.where(x > b, live[b], 0)
    shape = (2 * tokens, tokens)
    row = lax.broadcasted_iota(jnp.int32, shape, 0)
    column = lax.broadcasted_iota(jnp.int32, shape, 1)
    place = (row >> log2(2 * per) << log2(per)) + (row & (per - 1))
    hot = ((place - (off & (tokens - 1)) + tokens) & (tokens - 1)) == column
    is_up = (row & per) != 0
    first = jnp.where(hot & ~is_up, 1.0, 0.0).astype(BF16)
    second = jnp.where(hot & is_up, 1.0, 0.0).astype(BF16)
    send[...] = (contract(first, act[0], 1, 0) + contract(second, grad[0], 1, 0)).astype(BF16)


def terms_kernel(hid, nums, own, right, left, over_in, over_up, gain, gate, up, down, keep, send):
    core = nums[CORE]
    gain_wide = gain[...].astype(F32)
    for k in range(4):
        inputs, upstream = pick((own, right, left, over_in, over_up), k)
        n = inputs.shape[0]
        wide = inputs.astype(F32)
        squares = jnp.sum(wide * wide, axis=1, keepdims=True)
        sq_hi = squares.astype(BF16).astype(F32)
        scaled = (wide * gain_wide).astype(BF16)
        lane = lax.broadcasted_iota(jnp.int32, (n, WIDE), 1)
        first = contract(scaled, gate[...], 1, 1)
        first = jnp.where(lane == hid, sq_hi, jnp.where(lane == hid + 1, squares - sq_hi, first))
        parts = (
            first.astype(BF16),
            contract(scaled, up[...], 1, 1).astype(BF16),
            contract(upstream, down[...], 1, 1).astype(BF16),
        )
        at = (k % 2) * n

        def store(out):
            for i, part in enumerate(parts):
                out[at : at + n, i * WIDE : (i + 1) * WIDE] = part

        pl.when(core == k // 2)(functools.partial(store, keep))
        pl.when(core != k // 2)(functools.partial(store, send))


def pair_kernel(nums, keep, recv, *outs):
    own = outs[0].shape[0]
    for i, out in enumerate(outs):
        chunk = (nums[LINE] + i) & (len(outs) - 1)
        rows = pl.ds(pl.multiple_of(chunk * own, own), own)
        out[...] = (keep[rows, :].astype(F32) + recv[rows, :].astype(F32)).astype(BF16)


def point_kernel(hid, features, *refs):
    terms, out = refs[:-1], refs[-1]

    def total(i):
        s = slice(i * WIDE, (i + 1) * WIDE)
        return sum((t[:, s].astype(F32) for t in terms[1:]), terms[0][:, s].astype(F32))

    gate, up, hidden_grad = total(0), total(1), total(2)
    lane = lax.broadcasted_iota(jnp.int32, gate.shape, 1)
    squares = jnp.sum(jnp.where((lane == hid) | (lane == hid + 1), gate, 0.0), axis=1, keepdims=True)
    inv_rms = lax.rsqrt(squares / features + 1e-05)
    gate = jnp.where(lane < hid, gate, 0.0) * inv_rms
    up = up * inv_rms
    logistic = jax.nn.sigmoid(gate)
    swished = gate * logistic
    slopes = logistic * (1.0 + gate * (1.0 - logistic))
    hidden = swished * up
    d_gate = (hidden_grad * up * slopes).astype(BF16)
    d_up = (hidden_grad * swished).astype(BF16)
    inner = jnp.sum(d_gate.astype(F32) * gate + d_up.astype(F32) * up, axis=1, keepdims=True)
    lane = lax.broadcasted_iota(jnp.int32, (gate.shape[0], 4), 1)
    inv_hi = inv_rms.astype(BF16).astype(F32)
    in_hi = inner.astype(BF16).astype(F32)
    tail = jnp.where(
        lane == 0, inv_hi, jnp.where(lane == 1, inv_rms - inv_hi, jnp.where(lane == 2, in_hi, inner - in_hi))
    )
    out[:, :hid] = hidden[:, :hid].astype(BF16)
    out[:, hid : 2 * hid] = d_gate[:, :hid]
    out[:, 2 * hid : 3 * hid] = d_up[:, :hid]
    out[:, 3 * hid :] = tail.astype(BF16)


def rows_of(every, k, n):
    cores, own = 2, n // 2
    at = [(((k % 2) * 2 + j) * cores + k // 2) * own for j in range(2)]
    return jnp.concatenate([every[a : a + own, :] for a in at], axis=0)


def where_packed(nums, row, batches, tokens, per, nx, block, part):
    batch = row >> log2(tokens)
    slot = row & (tokens - 1)
    limit, off = jnp.zeros_like(row), jnp.zeros_like(row)
    for b in range(batches):
        limit = jnp.where(batch == b, nums[LIVE + b], limit)
        off = jnp.where(batch == b, nums[LIVE + batches + b], off)
    at = off + slot
    device = (at & (tokens - 1)) >> log2(per)
    turn = (device - nums[REPLICA] + nx) & (nx - 1)
    held = jnp.where(turn == nx - 1, 1, jnp.where(turn == 1, 2, jnp.where(turn == 2, 3, 0)))
    index = held * part + (device >> log2(nx)) * block + (at >> log2(tokens)) * per + (at & (per - 1))
    return jnp.where(slot < limit, index, -1)


def term_kernel(
    hid, features, plan, nums, own, right, left, over_in, over_up, every, gain, gate, up,
    out, up_own, term_ref,
):
    nx = out.shape[0]
    gain_wide = gain[...].astype(F32)
    gain_term = jnp.zeros(gain_wide.shape, F32)
    own_rows = up_own.shape[0]
    own_total = jnp.zeros(up_own.shape, F32)
    row = nums[ME] * own_rows + lax.broadcasted_iota(jnp.int32, (own_rows, 1), 0)
    index = where_packed(nums, row, *plan)
    for k in range(4):
        inputs, upstream = pick((own, right, left, over_in, over_up), k)
        n = inputs.shape[0]
        pay = rows_of(every, k, n)
        tail = pay[:, 3 * hid :].astype(F32)
        inv_rms = tail[:, 0:1] + tail[:, 1:2]
        inner = tail[:, 2:3] + tail[:, 3:4]
        d_normed = contract(pay[:, hid : 2 * hid], gate[...], 1, 0) + contract(
            pay[:, 2 * hid : 3 * hid], up[...], 1, 0
        )
        unit = inputs.astype(F32) * inv_rms
        gain_term = gain_term + jnp.sum(d_normed * unit, axis=0, keepdims=True)
        term = inv_rms * (gain_wide * d_normed - unit * (inner / features))
        term_ref[k * n : (k + 1) * n, :] = term.astype(BF16)
        column = lax.broadcasted_iota(jnp.int32, (own_rows, n), 1) + k * n
        hot = jnp.where(index == column, 1.0, 0.0).astype(BF16)
        own_total = own_total + contract(hot, upstream, 1, 0)
    up_own[...] = own_total.astype(BF16)
    gain_hi = gain_term.astype(BF16).astype(F32)
    rows = plan[0] * plan[1] // nx
    extra = out.shape[1] - rows
    row = lax.broadcasted_iota(jnp.int32, (extra, gain_term.shape[1]), 0)
    extras = jnp.where(row == 0, gain_hi, jnp.where(row == 1, gain_term - gain_hi, 0.0)).astype(BF16)
    live = term_ref.shape[0]
    column = lax.broadcasted_iota(jnp.int32, (rows, live), 1)
    i = lax.broadcasted_iota(jnp.int32, (rows, 1), 0)
    for q in range(nx):
        row = (((i >> log2(own_rows)) * nx + q) << log2(own_rows)) + (i & (own_rows - 1))
        hot = jnp.where(where_packed(nums, row, *plan) == column, 1.0, 0.0).astype(BF16)
        out[q, :rows, :] = contract(hot, term_ref[...], 1, 0).astype(BF16)
        out[q, rows:, :] = extras


def grads_kernel(
    hid, own, right, left, over_in, over_up, every, gain,
    grad_gate, grad_up, grad_down, pay_ref, normed_ref, up_ref,
):
    gain_wide = gain[...].astype(F32)
    for k in range(4):
        inputs, upstream = pick((own, right, left, over_in, over_up), k)
        n = inputs.shape[0]
        s = slice(k * n, (k + 1) * n)
        pay = rows_of(every, k, n)
        tail = pay[:, 3 * hid :].astype(F32)
        inv_rms = tail[:, 0:1] + tail[:, 1:2]
        for i in range(3):
            pay_ref[i, s, :hid] = pay[:, i * hid : (i + 1) * hid]
        normed_ref[s, :] = (inputs.astype(F32) * inv_rms * gain_wide).astype(BF16)
        up_ref[s, :] = upstream
    grad_down[...] = contract(pay_ref[0, :, :hid], up_ref[...], 0, 0).astype(BF16)
    normed = normed_ref[...]
    grad_gate[...] = contract(pay_ref[1, :, :hid], normed, 0, 0).astype(BF16)
    grad_up[...] = contract(pay_ref[2, :, :hid], normed, 0, 0).astype(BF16)


def middle_kernel(parts, out):
    sections, own_rows, lanes = out.shape
    width = parts.shape[2]
    rows = sections * own_rows
    total = parts[0].astype(F32)
    for r in range(1, parts.shape[0]):
        total = total + parts[r].astype(F32)
    out[:, :, :width] = total[:rows].astype(BF16).reshape(sections, own_rows, width)
    gain = total[rows : rows + 1] + total[rows + 1 : rows + 2]
    row = lax.broadcasted_iota(jnp.int32, (own_rows, 128), 0)
    tile = jnp.zeros((own_rows, 128), F32)
    for i in range(width // 128):
        tile = jnp.where(row == i, gain[:, i * 128 : (i + 1) * 128], tile)
    tile = tile.astype(BF16)
    for s in range(sections):
        out[s, :, width:] = tile


def final_kernel(parts, up_own, d_input, grad_gain):
    width = up_own.shape[1]
    total = parts[0].astype(F32)
    for r in range(1, parts.shape[0]):
        total = total + parts[r].astype(F32)
    d_input[...] = (up_own[...].astype(F32) + total[:, :width]).astype(BF16)
    for i in range(width // 128):
        grad_gain[:, i * 128 : (i + 1) * 128] = total[i : i + 1, width:]


def per_device(
    act_log, grad_log, failed_section, live_tokens, gate_weight, up_weight, down_weight, norm_gain
):
    ny, nzh, nx = (lax.axis_size(a) for a in ROWS_AXES)
    nzl, nc = lax.axis_size("zl"), lax.axis_size("c")
    sections = ny * nzh
    shards = sections * nx
    tokens, width = act_log.shape[1:]
    batches = live_tokens.shape[0]
    rows = batches * tokens
    live = 3 * rows // 4
    per = tokens // (ny * nx)
    cycles = live // tokens
    features = float(width * nzl * nc)
    hid = gate_weight.shape[1]
    failed = failed_section[0]
    source = (failed + sections - 1) % sections
    target = (failed + 1) % sections
    batch = jnp.arange(batches, dtype=jnp.int32)
    offs = jnp.sum(jnp.where(batch[None, :] < batch[:, None], live_tokens[None, :], 0), axis=1)
    x = lax.axis_index("x")
    me = lax.axis_index(ROWS_AXES)
    plan = (batches, tokens, per, nx, cycles * per, ny * cycles * per)

    def shape(*dims, dtype=BF16):
        return jax.ShapeDtypeStruct(dims, dtype)

    nums = jnp.stack([lax.axis_index("c"), x, me, lax.axis_index("zl")]).astype(jnp.int32)
    nums = jnp.concatenate([nums, live_tokens, offs.astype(jnp.int32)])
    send = call(
        functools.partial(scatter_kernel, per), shape(2 * tokens, width), [],
        4 * tokens * tokens * width, live_tokens, act_log, grad_log,
    )
    recv = lax.all_to_all(send, ("y", "x"), 0, 0, tiled=True).reshape(ny * nx, 2 * per, width)
    got = jnp.stack(
        [
            lax.dynamic_slice_in_dim(recv, source // nzh * nx, nx, 0)[:, :per],
            lax.dynamic_slice_in_dim(recv, target // nzh * nx, nx, 0)[:, per:],
        ]
    )
    place = lax.axis_index(("y", "x")) * per + jnp.arange(per, dtype=jnp.int32)
    slot = (place[None, :] - offs[:, None]) % tokens
    cycle = (offs[:, None] + slot) // tokens
    hit = (slot < live_tokens[:, None])[:, None, :] & (
        cycle[:, None, :] == jnp.arange(cycles, dtype=jnp.int32)[None, :, None]
    )
    packed = jnp.sum(
        jnp.where(hit[None, :, :, :, None], got[:, :, None].astype(F32), 0.0), axis=1
    ).astype(BF16)
    block = cycles * per
    packed = packed.reshape(2 * block, width)

    other = lax.ppermute(packed, "zh", [(0, 1), (1, 0)])
    packed = jnp.where(lax.axis_index("zh") == source % nzh, packed, other)

    copies = jnp.broadcast_to(packed[None], (ny,) + packed.shape).reshape(-1, width)
    column = lax.all_to_all(copies, "y", 0, 0, tiled=True)
    part = ny * block
    out_row = lax.broadcasted_iota(jnp.int32, (2 * part, 2 * part), 0)
    from_row = lax.broadcasted_iota(jnp.int32, (2 * part, 2 * part), 1)
    at = out_row % part
    hot = (at // block * 2 + out_row // part) * block + at % block == from_row
    own = contract(hot.astype(BF16), column, 1, 0).astype(BF16).reshape(2, part, width)
    ahead = [(i, (i + 1) % nx) for i in range(nx)]
    back = [(i, (i - 1) % nx) for i in range(nx)]
    right = lax.ppermute(own, "x", ahead)
    left = lax.ppermute(own, "x", back)
    over_in = lax.ppermute(right[0], "x", ahead)
    over_up = lax.ppermute(left[1], "x", back)
    blocks = (own, right, left, over_in, over_up)

    pad = ((0, WIDE - hid), (0, 0))
    gate_rows, up_rows = gate_weight.T, up_weight.T
    gate_pad, up_pad, down_pad = (jnp.pad(w, pad) for w in (gate_rows, up_rows, down_weight))
    gain = norm_gain.reshape(1, width)
    lanes = 3 * WIDE
    half = live // nc
    own_count = half // nzl

    product = 2 * live * width * WIDE
    keep, give = call(
        functools.partial(terms_kernel, hid), (shape(half, lanes), shape(half, lanes)), [], 3 * product,
        nums, *blocks, gain, gate_pad, up_pad, down_pad,
    )
    taken = lax.ppermute(give, "c", [(0, 1), (1, 0)])
    chunk = shape(own_count, lanes)
    pairs = call(pair_kernel, (chunk,) * nzl, [], half * lanes, nums, keep, taken)
    others = [
        lax.ppermute(pairs[i], "zl", [(a, (a + i) % nzl) for a in range(nzl)]) for i in range(1, nzl)
    ]
    point = call(
        functools.partial(point_kernel, hid, features), shape(own_count, 3 * hid + 4), [],
        20 * own_count * lanes, pairs[0], *others,
    )
    every = lax.all_gather(point, ("zl", "c"), axis=0, tiled=True)

    own_rows = rows // shards
    count = rows // nx
    out, up_own = call(
        functools.partial(term_kernel, hid, features, plan),
        (shape(nx, count + 16, width), shape(own_rows, width)),
        [pltpu.VMEM((live, width), BF16)],
        5 * product,
        nums, *blocks, every, gain, gate_rows, up_rows,
    )
    out = lax.all_to_all(out, "x", 0, 0, tiled=True)
    out = call(
        middle_kernel, shape(sections, own_rows, width + 128), [], nx * count * width, out
    )
    out = lax.all_to_all(out, ("y", "zh"), 0, 0, tiled=True)
    d_input, grad_gain = call(
        final_kernel, (shape(own_rows, width), shape(1, width, dtype=F32)), [],
        sections * own_rows * width, out, up_own,
    )

    grad_gate, grad_up, grad_down = call(
        functools.partial(grads_kernel, hid),
        (shape(hid, width),) * 3,
        [
            pltpu.VMEM((3, live, WIDE), BF16),
            pltpu.VMEM((live, width), BF16),
            pltpu.VMEM((live, width), BF16),
        ],
        3 * product,
        *blocks, every, gain,
    )
    return (d_input, grad_gate.T, grad_up.T, grad_down, grad_gain.reshape(width))


def solution(mesh):
    fine = Mesh(mesh.devices.reshape(8, 2, 4, 4, 2), AXES)
    section, replica, tensor = ("y", "zh"), "x", ("zl", "c")
    split = ("y", "zh", "x")
    in_specs = (
        P(section, replica, tensor),
        P(section, replica, tensor),
        P(),
        P(),
        P(tensor, split),
        P(tensor, split),
        P(split, tensor),
        P(tensor),
    )
    out_specs = (
        P(split, tensor),
        P(tensor, split),
        P(tensor, split),
        P(split, tensor),
        P(tensor),
    )
    return jax.shard_map(
        per_device, mesh=fine, in_specs=in_specs, out_specs=out_specs, check_vma=False
    )
```

```python
import functools

import jax
import jax.numpy as jnp
from jax import lax
from jax.experimental import pallas as pl
from jax.experimental.pallas import tpu as pltpu
from jax.sharding import Mesh, PartitionSpec as P

AXES = ("y", "zh", "x", "zl", "c")
ROWS_AXES = ("y", "zh", "x")
F32 = jnp.float32
BF16 = jnp.bfloat16
WIDE = 256
VMEM = pl.BlockSpec(memory_space=pltpu.VMEM)
SMEM = pl.BlockSpec(memory_space=pltpu.SMEM)


def contract(left, right, l, r):
    return lax.dot_general(left, right, (((l,), (r,)), ((), ())), preferred_element_type=F32)


def call(body, outs, scratch, flops, *args):
    moved = sum(a.size * a.dtype.itemsize for a in args) + sum(
        o.size * o.dtype.itemsize for o in jax.tree.leaves(outs)
    )
    return pl.pallas_call(
        body,
        out_shape=outs,
        in_specs=[SMEM if a.ndim == 1 else VMEM for a in args],
        out_specs=jax.tree.map(lambda _: VMEM, outs),
        scratch_shapes=scratch,
        compiler_params=pltpu.CompilerParams(vmem_limit_bytes=48 * 1024 * 1024),
        cost_estimate=pl.CostEstimate(flops=flops, bytes_accessed=moved, transcendentals=0),
    )(*args)


def pick(refs, k):
    own, right, left, over_in, over_up = refs
    if k < 3:
        ref = (own, right, left)[k]
        return ref[0], ref[1]
    return over_in[...], over_up[...]


def log2(n):
    assert n & (n - 1) == 0
    return n.bit_length() - 1


CORE, REPLICA, ME, LINE, LIVE = 0, 1, 2, 3, 4


def scatter_kernel(per, live, act, grad, send):
    tokens = act.shape[1]
    x = lax.axis_index("x")
    off = jnp.int32(0)
    for b in range(live.shape[0] - 1):
        off = off + jnp.where(x > b, live[b], 0)
    shape = (2 * tokens, tokens)
    row = lax.broadcasted_iota(jnp.int32, shape, 0)
    column = lax.broadcasted_iota(jnp.int32, shape, 1)
    place = (row >> log2(2 * per) << log2(per)) + (row & (per - 1))
    hot = ((place - (off & (tokens - 1)) + tokens) & (tokens - 1)) == column
    is_up = (row & per) != 0
    first = jnp.where(hot & ~is_up, 1.0, 0.0).astype(BF16)
    second = jnp.where(hot & is_up, 1.0, 0.0).astype(BF16)
    send[...] = (contract(first, act[0], 1, 0) + contract(second, grad[0], 1, 0)).astype(BF16)


TAIL = 16


def terms_kernel(nums, own, right, left, over_in, over_up, gain, ahead, behind, rest, keep, send):
    core = nums[CORE]
    gain_wide = gain[...].astype(F32)
    n = over_in.shape[0]
    chunk = n // 2
    ones = jnp.ones(rest.shape, BF16)
    for k in range(4):
        inputs, upstream = pick((own, right, left, over_in, over_up), k)
        wide = inputs.astype(F32)
        scaled = (wide * gain_wide).astype(BF16)
        main = contract(scaled, ahead[...], 1, 1) + contract(upstream, behind[...], 1, 1)
        main = main.astype(BF16)
        squares = wide * wide
        high = squares.astype(BF16)
        low = (squares - high.astype(F32)).astype(BF16)
        tails = []
        for h in range(2):
            r = slice(h * chunk, (h + 1) * chunk)
            total = contract(ones, high[r], 1, 1) + contract(ones, low[r], 1, 1)
            total_hi = total.astype(BF16).astype(F32)
            row = lax.broadcasted_iota(jnp.int32, total.shape, 0)
            total = jnp.where(row == 0, total_hi, jnp.where(row == 1, total - total_hi, 0.0))
            tails.append(jnp.concatenate([contract(rest[...], upstream[r], 1, 1), total], axis=0).astype(BF16))

        def store(out):
            for h in range(2):
                at = (k % 2) * 2 + h
                for i in range(main.shape[1] // 128):
                    out[at, i * chunk : (i + 1) * chunk, :] = main[
                        h * chunk : (h + 1) * chunk, i * 128 : (i + 1) * 128
                    ]
                out[at, -TAIL:, :] = jnp.zeros((TAIL, 128), BF16)
                out[at, -TAIL:, :chunk] = tails[h]

        pl.when(core == k // 2)(functools.partial(store, keep))
        pl.when(core != k // 2)(functools.partial(store, send))


def pair_kernel(nums, keep, recv, *outs):
    for i, out in enumerate(outs):
        chunk = (nums[LINE] + i) & (len(outs) - 1)
        out[...] = (keep[chunk].astype(F32) + recv[chunk].astype(F32)).astype(BF16)


def point_kernel(hid, features, *refs):
    terms, (out, main_ref, hg_ref, tail_ref) = refs[:-4], refs[-4:]
    rows, width = main_ref.shape
    total = terms[0][...].astype(F32)
    for t in terms[1:]:
        total = total + t[...].astype(F32)
    for i in range(width // 128):
        main_ref[:, i * 128 : (i + 1) * 128] = total[i * rows : (i + 1) * rows]
    tail = total[-TAIL:].T[:rows]
    inside = width - 2 * hid
    gate = main_ref[:, :hid]
    up = main_ref[:, hid : 2 * hid]
    hg_ref[:, :inside] = main_ref[:, 2 * hid :]
    hg_ref[:, inside:] = tail[:, : hid - inside]
    hidden_grad = hg_ref[...]
    squares = tail[:, hid - inside : hid - inside + 1] + tail[:, hid - inside + 1 : hid - inside + 2]
    inv_rms = lax.rsqrt(squares / features + 1e-05)
    gate = gate * inv_rms
    up = up * inv_rms
    logistic = jax.nn.sigmoid(gate)
    swished = gate * logistic
    slopes = logistic * (1.0 + gate * (1.0 - logistic))
    d_gate = (hidden_grad * up * slopes).astype(BF16).astype(F32)
    d_up = (hidden_grad * swished).astype(BF16).astype(F32)
    inner = jnp.sum(d_gate * gate + d_up * up, axis=1, keepdims=True)
    main_ref[:, :hid] = swished * up
    main_ref[:, hid : 2 * hid] = d_gate
    main_ref[:, 2 * hid :] = d_up[:, :inside]
    inv_hi = inv_rms.astype(BF16).astype(F32)
    in_hi = inner.astype(BF16).astype(F32)
    tail_ref[...] = jnp.zeros(tail_ref.shape, F32)
    tail_ref[:rows, : hid - inside] = d_up[:, inside:]
    for i, v in enumerate((inv_hi, inv_rms - inv_hi, in_hi, inner - in_hi)):
        at = hid - inside + i
        tail_ref[:rows, at : at + 1] = v
    for i in range(width // 128):
        out[i * rows : (i + 1) * rows, :] = main_ref[:, i * 128 : (i + 1) * 128].astype(BF16)
    out[-TAIL:, :] = tail_ref[...].T[:TAIL].astype(BF16)


def rows_of(every, k, n, hid, width, pay_ref):
    own = n // 2
    pieces = width // 128
    size = pieces * own + TAIL
    inside = width - 2 * hid
    tails = []
    for j in range(2):
        at = (((k % 2) * 2 + j) * 2 + k // 2) * size
        r = slice(k * n + j * own, k * n + (j + 1) * own)
        main = jnp.concatenate(
            [every[at + i * own : at + (i + 1) * own, :] for i in range(pieces)], axis=1
        )
        tail = every[at + pieces * own : at + size, :].astype(F32).T[:own]
        pay_ref[0, r, :hid] = main[:, :hid]
        pay_ref[1, r, :hid] = main[:, hid : 2 * hid]
        pay_ref[2, r, :inside] = main[:, 2 * hid :]
        pay_ref[2, r, inside:hid] = tail[:, : hid - inside].astype(BF16)
        tails.append(tail[:, hid - inside :])
    tail = jnp.concatenate(tails, axis=0)
    return tail[:, 0:1] + tail[:, 1:2], tail[:, 2:3] + tail[:, 3:4]


def where_packed(nums, row, batches, tokens, per, nx, block, part):
    batch = row >> log2(tokens)
    slot = row & (tokens - 1)
    limit, off = jnp.zeros_like(row), jnp.zeros_like(row)
    for b in range(batches):
        limit = jnp.where(batch == b, nums[LIVE + b], limit)
        off = jnp.where(batch == b, nums[LIVE + batches + b], off)
    at = off + slot
    device = (at & (tokens - 1)) >> log2(per)
    turn = (device - nums[REPLICA] + nx) & (nx - 1)
    held = jnp.where(turn == nx - 1, 1, jnp.where(turn == 1, 2, jnp.where(turn == 2, 3, 0)))
    index = held * part + (device >> log2(nx)) * block + (at >> log2(tokens)) * per + (at & (per - 1))
    return jnp.where(slot < limit, index, -1)


def term_kernel(
    hid, features, plan, nums, own, right, left, over_in, over_up, every, gain, gate, up,
    out, up_own, term_ref, pay_ref,
):
    nx = out.shape[0]
    gain_wide = gain[...].astype(F32)
    gain_term = jnp.zeros(gain_wide.shape, F32)
    own_rows = up_own.shape[0]
    own_total = jnp.zeros(up_own.shape, F32)
    row = nums[ME] * own_rows + lax.broadcasted_iota(jnp.int32, (own_rows, 1), 0)
    index = where_packed(nums, row, *plan)
    for k in range(4):
        inputs, upstream = pick((own, right, left, over_in, over_up), k)
        n = inputs.shape[0]
        s = slice(k * n, (k + 1) * n)
        inv_rms, inner = rows_of(every, k, n, hid, inputs.shape[1], pay_ref)
        d_normed = contract(pay_ref[1, s, :hid], gate[...], 1, 0) + contract(
            pay_ref[2, s, :hid], up[...], 1, 0
        )
        unit = inputs.astype(F32) * inv_rms
        gain_term = gain_term + jnp.sum(d_normed * unit, axis=0, keepdims=True)
        term = inv_rms * (gain_wide * d_normed - unit * (inner / features))
        term_ref[s, :] = term.astype(BF16)
        column = lax.broadcasted_iota(jnp.int32, (own_rows, n), 1) + k * n
        hot = jnp.where(index == column, 1.0, 0.0).astype(BF16)
        own_total = own_total + contract(hot, upstream, 1, 0)
    up_own[...] = own_total.astype(BF16)
    gain_hi = gain_term.astype(BF16).astype(F32)
    rows = plan[0] * plan[1] // nx
    extra = out.shape[1] - rows
    row = lax.broadcasted_iota(jnp.int32, (extra, gain_term.shape[1]), 0)
    extras = jnp.where(row == 0, gain_hi, jnp.where(row == 1, gain_term - gain_hi, 0.0)).astype(BF16)
    live = term_ref.shape[0]
    column = lax.broadcasted_iota(jnp.int32, (rows, live), 1)
    i = lax.broadcasted_iota(jnp.int32, (rows, 1), 0)
    for q in range(nx):
        row = (((i >> log2(own_rows)) * nx + q) << log2(own_rows)) + (i & (own_rows - 1))
        hot = jnp.where(where_packed(nums, row, *plan) == column, 1.0, 0.0).astype(BF16)
        out[q, :rows, :] = contract(hot, term_ref[...], 1, 0).astype(BF16)
        out[q, rows:, :] = extras


def grads_kernel(
    hid, own, right, left, over_in, over_up, every, gain,
    grad_gate, grad_up, grad_down, pay_ref, normed_ref, up_ref,
):
    gain_wide = gain[...].astype(F32)
    for k in range(4):
        inputs, upstream = pick((own, right, left, over_in, over_up), k)
        n = inputs.shape[0]
        s = slice(k * n, (k + 1) * n)
        inv_rms, _ = rows_of(every, k, n, hid, inputs.shape[1], pay_ref)
        normed_ref[s, :] = (inputs.astype(F32) * inv_rms * gain_wide).astype(BF16)
        up_ref[s, :] = upstream
    grad_down[...] = contract(pay_ref[0, :, :hid], up_ref[...], 0, 0).astype(BF16)
    normed = normed_ref[...]
    grad_gate[...] = contract(pay_ref[1, :, :hid], normed, 0, 0).astype(BF16)
    grad_up[...] = contract(pay_ref[2, :, :hid], normed, 0, 0).astype(BF16)


def middle_kernel(parts, out):
    sections, own_rows, lanes = out.shape
    width = parts.shape[2]
    rows = sections * own_rows
    total = parts[0].astype(F32)
    for r in range(1, parts.shape[0]):
        total = total + parts[r].astype(F32)
    out[:, :, :width] = total[:rows].astype(BF16).reshape(sections, own_rows, width)
    gain = total[rows : rows + 1] + total[rows + 1 : rows + 2]
    row = lax.broadcasted_iota(jnp.int32, (own_rows, 128), 0)
    tile = jnp.zeros((own_rows, 128), F32)
    for i in range(width // 128):
        tile = jnp.where(row == i, gain[:, i * 128 : (i + 1) * 128], tile)
    tile = tile.astype(BF16)
    for s in range(sections):
        out[s, :, width:] = tile


def final_kernel(parts, up_own, d_input, grad_gain):
    width = up_own.shape[1]
    total = parts[0].astype(F32)
    for r in range(1, parts.shape[0]):
        total = total + parts[r].astype(F32)
    d_input[...] = (up_own[...].astype(F32) + total[:, :width]).astype(BF16)
    for i in range(width // 128):
        grad_gain[:, i * 128 : (i + 1) * 128] = total[i : i + 1, width:]


def per_device(
    act_log, grad_log, failed_section, live_tokens, gate_weight, up_weight, down_weight, norm_gain
):
    ny, nzh, nx = (lax.axis_size(a) for a in ROWS_AXES)
    nzl, nc = lax.axis_size("zl"), lax.axis_size("c")
    sections = ny * nzh
    shards = sections * nx
    tokens, width = act_log.shape[1:]
    batches = live_tokens.shape[0]
    rows = batches * tokens
    live = 3 * rows // 4
    per = tokens // (ny * nx)
    cycles = live // tokens
    features = float(width * nzl * nc)
    hid = gate_weight.shape[1]
    failed = failed_section[0]
    source = (failed + sections - 1) % sections
    target = (failed + 1) % sections
    batch = jnp.arange(batches, dtype=jnp.int32)
    offs = jnp.sum(jnp.where(batch[None, :] < batch[:, None], live_tokens[None, :], 0), axis=1)
    x = lax.axis_index("x")
    me = lax.axis_index(ROWS_AXES)
    plan = (batches, tokens, per, nx, cycles * per, ny * cycles * per)

    def shape(*dims, dtype=BF16):
        return jax.ShapeDtypeStruct(dims, dtype)

    nums = jnp.stack([lax.axis_index("c"), x, me, lax.axis_index("zl")]).astype(jnp.int32)
    nums = jnp.concatenate([nums, live_tokens, offs.astype(jnp.int32)])
    send = call(
        functools.partial(scatter_kernel, per), shape(2 * tokens, width), [],
        4 * tokens * tokens * width, live_tokens, act_log, grad_log,
    )
    recv = lax.all_to_all(send, ("y", "x"), 0, 0, tiled=True).reshape(ny * nx, 2 * per, width)
    got = jnp.stack(
        [
            lax.dynamic_slice_in_dim(recv, source // nzh * nx, nx, 0)[:, :per],
            lax.dynamic_slice_in_dim(recv, target // nzh * nx, nx, 0)[:, per:],
        ]
    )
    place = lax.axis_index(("y", "x")) * per + jnp.arange(per, dtype=jnp.int32)
    slot = (place[None, :] - offs[:, None]) % tokens
    cycle = (offs[:, None] + slot) // tokens
    hit = (slot < live_tokens[:, None])[:, None, :] & (
        cycle[:, None, :] == jnp.arange(cycles, dtype=jnp.int32)[None, :, None]
    )
    packed = jnp.sum(
        jnp.where(hit[None, :, :, :, None], got[:, :, None].astype(F32), 0.0), axis=1
    ).astype(BF16)
    block = cycles * per
    packed = packed.reshape(2 * block, width)

    other = lax.ppermute(packed, "zh", [(0, 1), (1, 0)])
    packed = jnp.where(lax.axis_index("zh") == source % nzh, packed, other)

    copies = jnp.broadcast_to(packed[None], (ny,) + packed.shape).reshape(-1, width)
    column = lax.all_to_all(copies, "y", 0, 0, tiled=True)
    part = ny * block
    out_row = lax.broadcasted_iota(jnp.int32, (2 * part, 2 * part), 0)
    from_row = lax.broadcasted_iota(jnp.int32, (2 * part, 2 * part), 1)
    at = out_row % part
    hot = (at // block * 2 + out_row // part) * block + at % block == from_row
    own = contract(hot.astype(BF16), column, 1, 0).astype(BF16).reshape(2, part, width)
    forth = [(i, (i + 1) % nx) for i in range(nx)]
    back = [(i, (i - 1) % nx) for i in range(nx)]
    right = lax.ppermute(own, "x", forth)
    left = lax.ppermute(own, "x", back)
    over_in = lax.ppermute(right[0], "x", forth)
    over_up = lax.ppermute(left[1], "x", back)
    blocks = (own, right, left, over_in, over_up)

    inside = width - 2 * hid
    gate_rows, up_rows = gate_weight.T, up_weight.T
    ahead_rows = jnp.concatenate([gate_rows, up_rows, jnp.zeros((inside, width), BF16)], axis=0)
    behind_rows = jnp.concatenate([jnp.zeros((2 * hid, width), BF16), down_weight[:inside]], axis=0)
    rest_rows = down_weight[inside:]
    gain = norm_gain.reshape(1, width)
    own_count = live // nc // nzl
    size = own_count * (width // 128) + TAIL
    product = 2 * live * width * WIDE
    halves = shape(nzl, size, 128)
    keep, give = call(
        terms_kernel, (halves, halves), [], 5 * product,
        nums, *blocks, gain, ahead_rows, behind_rows, rest_rows,
    )
    taken = lax.ppermute(give, "c", [(0, 1), (1, 0)])
    chunk = shape(size, 128)
    pairs = call(pair_kernel, (chunk,) * nzl, [], nzl * size * 128, nums, keep, taken)
    others = [
        lax.ppermute(pairs[i], "zl", [(a, (a + i) % nzl) for a in range(nzl)]) for i in range(1, nzl)
    ]
    point = call(
        functools.partial(point_kernel, hid, features), chunk,
        [
            pltpu.VMEM((own_count, width), F32),
            pltpu.VMEM((own_count, hid), F32),
            pltpu.VMEM((128, 128), F32),
        ],
        20 * size * 128, pairs[0], *others,
    )
    every = lax.all_gather(point, ("zl", "c"), axis=0, tiled=True)

    own_rows = rows // shards
    count = rows // nx
    out, up_own = call(
        functools.partial(term_kernel, hid, features, plan),
        (shape(nx, count + 16, width), shape(own_rows, width)),
        [pltpu.VMEM((live, width), BF16), pltpu.VMEM((3, live, WIDE), BF16)],
        5 * product,
        nums, *blocks, every, gain, gate_rows, up_rows,
    )
    out = lax.all_to_all(out, "x", 0, 0, tiled=True)
    out = call(
        middle_kernel, shape(sections, own_rows, width + 128), [], nx * count * width, out
    )
    out = lax.all_to_all(out, ("y", "zh"), 0, 0, tiled=True)
    d_input, grad_gain = call(
        final_kernel, (shape(own_rows, width), shape(1, width, dtype=F32)), [],
        sections * own_rows * width, out, up_own,
    )

    grad_gate, grad_up, grad_down = call(
        functools.partial(grads_kernel, hid),
        (shape(hid, width),) * 3,
        [
            pltpu.VMEM((3, live, WIDE), BF16),
            pltpu.VMEM((live, width), BF16),
            pltpu.VMEM((live, width), BF16),
        ],
        3 * product,
        *blocks, every, gain,
    )
    return (d_input, grad_gate.T, grad_up.T, grad_down, grad_gain.reshape(width))


def solution(mesh):
    fine = Mesh(mesh.devices.reshape(8, 2, 4, 4, 2), AXES)
    section, replica, tensor = ("y", "zh"), "x", ("zl", "c")
    split = ("y", "zh", "x")
    in_specs = (
        P(section, replica, tensor),
        P(section, replica, tensor),
        P(),
        P(),
        P(tensor, split),
        P(tensor, split),
        P(split, tensor),
        P(tensor),
    )
    out_specs = (
        P(split, tensor),
        P(tensor, split),
        P(tensor, split),
        P(split, tensor),
        P(tensor),
    )
    return jax.shard_map(
        per_device, mesh=fine, in_specs=in_specs, out_specs=out_specs, check_vma=False
    )
```

```python
import functools

import jax
import jax.numpy as jnp
from jax import lax
from jax.experimental import pallas as pl
from jax.experimental.pallas import tpu as pltpu
from jax.sharding import Mesh, PartitionSpec as P

AXES = ("y", "zh", "x", "zl", "c")
ROWS_AXES = ("y", "zh", "x")
F32 = jnp.float32
BF16 = jnp.bfloat16
WIDE = 256
VMEM = pl.BlockSpec(memory_space=pltpu.VMEM)
SMEM = pl.BlockSpec(memory_space=pltpu.SMEM)
AWAY = pl.BlockSpec(memory_space=pl.ANY)


def contract(left, right, l, r):
    return lax.dot_general(left, right, (((l,), (r,)), ((), ())), preferred_element_type=F32)


def call(body, outs, scratch, flops, *args, away=()):
    moved = sum(a.size * a.dtype.itemsize for a in args) + sum(
        o.size * o.dtype.itemsize for o in jax.tree.leaves(outs)
    )
    return pl.pallas_call(
        body,
        out_shape=outs,
        in_specs=[
            SMEM if a.ndim == 1 else AWAY if i in away else VMEM for i, a in enumerate(args)
        ],
        out_specs=jax.tree.map(lambda _: VMEM, outs),
        scratch_shapes=scratch,
        compiler_params=pltpu.CompilerParams(vmem_limit_bytes=48 * 1024 * 1024),
        cost_estimate=pl.CostEstimate(flops=flops, bytes_accessed=moved, transcendentals=0),
    )(*args)


def pick(refs, k):
    own, right, left, over_in, over_up = refs
    if k < 3:
        ref = (own, right, left)[k]
        return ref[0], ref[1]
    return over_in[...], over_up[...]


def log2(n):
    assert n & (n - 1) == 0
    return n.bit_length() - 1


CORE, REPLICA, ME, LINE, LIVE = 0, 1, 2, 3, 4


COPIES = 4


def scatter_kernel(per, live, act, grad, send, act_ref, grad_ref, sems):
    tokens, width = act_ref.shape
    step = tokens // COPIES
    copies = []
    for i in range(COPIES):
        rows = pl.ds(i * step, step)
        for k, (source, dest) in enumerate(((act, act_ref), (grad, grad_ref))):
            copy = pltpu.make_async_copy(source.at[0, rows, :], dest.at[rows, :], sems.at[k, i])
            copy.start()
            copies.append(copy)
    x = lax.axis_index("x")
    off = jnp.int32(0)
    for b in range(live.shape[0] - 1):
        off = off + jnp.where(x > b, live[b], 0)
    row = lax.broadcasted_iota(jnp.int32, (tokens, tokens), 0)
    column = lax.broadcasted_iota(jnp.int32, (tokens, tokens), 1)
    roll = ((row - column - off) & (tokens - 1)) == 0
    roll = jnp.where(roll, 1.0, 0.0).astype(BF16)
    for copy in copies:
        copy.wait()
    groups = (tokens // per, per, width)
    first = contract(roll, act_ref[...], 1, 0).reshape(groups)
    second = contract(roll, grad_ref[...], 1, 0).reshape(groups)
    send[...] = jnp.concatenate([first, second], axis=1).reshape(2 * tokens, width).astype(BF16)


TAIL = 16


def terms_kernel(nums, own, right, left, over_in, over_up, gain, ahead, behind, rest, keep, send, tail_ref):
    core = nums[CORE]
    gain_wide = gain[...].astype(F32)
    n = over_in.shape[0]
    chunk = n // 2
    extra = rest.shape[0]
    tail_ref[...] = jnp.zeros(tail_ref.shape, F32)
    for k in range(4):
        inputs, upstream = pick((own, right, left, over_in, over_up), k)
        wide = inputs.astype(F32)
        scaled = (wide * gain_wide).astype(BF16)
        main = contract(scaled, ahead[...], 1, 1) + contract(upstream, behind[...], 1, 1)
        main = main.astype(BF16)
        squares = jnp.sum(wide * wide, axis=1, keepdims=True)
        high = squares.astype(BF16).astype(F32)
        at = slice(k * n, (k + 1) * n)
        tail_ref[at, :extra] = contract(upstream, rest[...], 1, 1)
        tail_ref[at, extra : extra + 1] = high
        tail_ref[at, extra + 1 : extra + 2] = squares - high
        tails = [
            tail_ref[k * n + h * chunk : k * n + (h + 1) * chunk, :].T[:TAIL].astype(BF16)
            for h in range(2)
        ]

        def store(out):
            for h in range(2):
                at = (k % 2) * 2 + h
                for i in range(main.shape[1] // 128):
                    out[at, i * chunk : (i + 1) * chunk, :] = main[
                        h * chunk : (h + 1) * chunk, i * 128 : (i + 1) * 128
                    ]
                out[at, -TAIL:, :] = jnp.zeros((TAIL, 128), BF16)
                out[at, -TAIL:, :chunk] = tails[h]

        pl.when(core == k // 2)(functools.partial(store, keep))
        pl.when(core != k // 2)(functools.partial(store, send))


def pair_kernel(nums, keep, recv, *outs):
    for i, out in enumerate(outs):
        chunk = (nums[LINE] + i) & (len(outs) - 1)
        out[...] = (keep[chunk].astype(F32) + recv[chunk].astype(F32)).astype(BF16)


def point_kernel(hid, features, *refs):
    terms, (out, main_ref, hg_ref, tail_ref) = refs[:-4], refs[-4:]
    rows, width = main_ref.shape
    total = terms[0][...].astype(F32)
    for t in terms[1:]:
        total = total + t[...].astype(F32)
    for i in range(width // 128):
        main_ref[:, i * 128 : (i + 1) * 128] = total[i * rows : (i + 1) * rows]
    tail = total[-TAIL:].T[:rows]
    inside = width - 2 * hid
    gate = main_ref[:, :hid]
    up = main_ref[:, hid : 2 * hid]
    hg_ref[:, :inside] = main_ref[:, 2 * hid :]
    hg_ref[:, inside:] = tail[:, : hid - inside]
    hidden_grad = hg_ref[...]
    squares = tail[:, hid - inside : hid - inside + 1] + tail[:, hid - inside + 1 : hid - inside + 2]
    inv_rms = lax.rsqrt(squares / features + 1e-05)
    gate = gate * inv_rms
    up = up * inv_rms
    logistic = jax.nn.sigmoid(gate)
    swished = gate * logistic
    slopes = logistic * (1.0 + gate * (1.0 - logistic))
    d_gate = (hidden_grad * up * slopes).astype(BF16).astype(F32)
    d_up = (hidden_grad * swished).astype(BF16).astype(F32)
    inner = jnp.sum(d_gate * gate + d_up * up, axis=1, keepdims=True)
    main_ref[:, :hid] = swished * up
    main_ref[:, hid : 2 * hid] = d_gate
    main_ref[:, 2 * hid :] = d_up[:, :inside]
    inv_hi = inv_rms.astype(BF16).astype(F32)
    in_hi = inner.astype(BF16).astype(F32)
    tail_ref[...] = jnp.zeros(tail_ref.shape, F32)
    tail_ref[:rows, : hid - inside] = d_up[:, inside:]
    for i, v in enumerate((inv_hi, inv_rms - inv_hi, in_hi, inner - in_hi)):
        at = hid - inside + i
        tail_ref[:rows, at : at + 1] = v
    for i in range(width // 128):
        out[i * rows : (i + 1) * rows, :] = main_ref[:, i * 128 : (i + 1) * 128].astype(BF16)
    out[-TAIL:, :] = tail_ref[...].T[:TAIL].astype(BF16)


def rows_of(every, k, n, hid, width, pay_ref):
    own = n // 2
    pieces = width // 128
    size = pieces * own + TAIL
    inside = width - 2 * hid
    tails = []
    for j in range(2):
        at = (((k % 2) * 2 + j) * 2 + k // 2) * size
        r = slice(k * n + j * own, k * n + (j + 1) * own)
        main = jnp.concatenate(
            [every[at + i * own : at + (i + 1) * own, :] for i in range(pieces)], axis=1
        )
        tail = every[at + pieces * own : at + size, :].astype(F32).T[:own]
        pay_ref[0, r, :hid] = main[:, :hid]
        pay_ref[1, r, :hid] = main[:, hid : 2 * hid]
        pay_ref[2, r, :inside] = main[:, 2 * hid :]
        pay_ref[2, r, inside:hid] = tail[:, : hid - inside].astype(BF16)
        tails.append(tail[:, hid - inside :])
    tail = jnp.concatenate(tails, axis=0)
    return tail[:, 0:1] + tail[:, 1:2], tail[:, 2:3] + tail[:, 3:4]


def where_packed(nums, row, batches, tokens, per, nx, block, part):
    batch = row >> log2(tokens)
    slot = row & (tokens - 1)
    limit, off = jnp.zeros_like(row), jnp.zeros_like(row)
    for b in range(batches):
        limit = jnp.where(batch == b, nums[LIVE + b], limit)
        off = jnp.where(batch == b, nums[LIVE + batches + b], off)
    at = off + slot
    device = (at & (tokens - 1)) >> log2(per)
    turn = (device - nums[REPLICA] + nx) & (nx - 1)
    held = jnp.where(turn == nx - 1, 1, jnp.where(turn == 1, 2, jnp.where(turn == 2, 3, 0)))
    index = held * part + (device >> log2(nx)) * block + (at >> log2(tokens)) * per + (at & (per - 1))
    return jnp.where(slot < limit, index, -1)


def term_kernel(
    hid, features, plan, nums, own, right, left, over_in, over_up, every, gain, gate, up,
    out, up_own, term_ref, pay_ref,
):
    nx = out.shape[0]
    gain_wide = gain[...].astype(F32)
    gain_term = jnp.zeros(gain_wide.shape, F32)
    own_rows = up_own.shape[0]
    own_total = jnp.zeros(up_own.shape, F32)
    row = nums[ME] * own_rows + lax.broadcasted_iota(jnp.int32, (own_rows, 1), 0)
    index = where_packed(nums, row, *plan)
    for k in range(4):
        inputs, upstream = pick((own, right, left, over_in, over_up), k)
        n = inputs.shape[0]
        s = slice(k * n, (k + 1) * n)
        inv_rms, inner = rows_of(every, k, n, hid, inputs.shape[1], pay_ref)
        d_normed = contract(pay_ref[1, s, :hid], gate[...], 1, 0) + contract(
            pay_ref[2, s, :hid], up[...], 1, 0
        )
        unit = inputs.astype(F32) * inv_rms
        gain_term = gain_term + jnp.sum(d_normed * unit, axis=0, keepdims=True)
        term = inv_rms * (gain_wide * d_normed - unit * (inner / features))
        term_ref[s, :] = term.astype(BF16)
        column = lax.broadcasted_iota(jnp.int32, (own_rows, n), 1) + k * n
        hot = jnp.where(index == column, 1.0, 0.0).astype(BF16)
        own_total = own_total + contract(hot, upstream, 1, 0)
    up_own[...] = own_total.astype(BF16)
    gain_hi = gain_term.astype(BF16).astype(F32)
    rows = plan[0] * plan[1] // nx
    extra = out.shape[1] - rows
    row = lax.broadcasted_iota(jnp.int32, (extra, gain_term.shape[1]), 0)
    extras = jnp.where(row == 0, gain_hi, jnp.where(row == 1, gain_term - gain_hi, 0.0)).astype(BF16)
    live = term_ref.shape[0]
    column = lax.broadcasted_iota(jnp.int32, (rows, live), 1)
    i = lax.broadcasted_iota(jnp.int32, (rows, 1), 0)
    for q in range(nx):
        row = (((i >> log2(own_rows)) * nx + q) << log2(own_rows)) + (i & (own_rows - 1))
        hot = jnp.where(where_packed(nums, row, *plan) == column, 1.0, 0.0).astype(BF16)
        out[q, :rows, :] = contract(hot, term_ref[...], 1, 0).astype(BF16)
        out[q, rows:, :] = extras


def grads_kernel(
    hid, own, right, left, over_in, over_up, every, gain,
    grad_gate, grad_up, grad_down, pay_ref, normed_ref, up_ref,
):
    gain_wide = gain[...].astype(F32)
    for k in range(4):
        inputs, upstream = pick((own, right, left, over_in, over_up), k)
        n = inputs.shape[0]
        s = slice(k * n, (k + 1) * n)
        inv_rms, _ = rows_of(every, k, n, hid, inputs.shape[1], pay_ref)
        normed_ref[s, :] = (inputs.astype(F32) * inv_rms * gain_wide).astype(BF16)
        up_ref[s, :] = upstream
    grad_down[...] = contract(pay_ref[0, :, :hid], up_ref[...], 0, 0).astype(BF16)
    normed = normed_ref[...]
    grad_gate[...] = contract(pay_ref[1, :, :hid], normed, 0, 0).astype(BF16)
    grad_up[...] = contract(pay_ref[2, :, :hid], normed, 0, 0).astype(BF16)


def middle_kernel(parts, out):
    sections, own_rows, lanes = out.shape
    width = parts.shape[2]
    rows = sections * own_rows
    total = parts[0].astype(F32)
    for r in range(1, parts.shape[0]):
        total = total + parts[r].astype(F32)
    out[:, :, :width] = total[:rows].astype(BF16).reshape(sections, own_rows, width)
    gain = total[rows : rows + 1] + total[rows + 1 : rows + 2]
    row = lax.broadcasted_iota(jnp.int32, (own_rows, 128), 0)
    tile = jnp.zeros((own_rows, 128), F32)
    for i in range(width // 128):
        tile = jnp.where(row == i, gain[:, i * 128 : (i + 1) * 128], tile)
    tile = tile.astype(BF16)
    for s in range(sections):
        out[s, :, width:] = tile


def final_kernel(parts, up_own, d_input, grad_gain):
    width = up_own.shape[1]
    total = parts[0].astype(F32)
    for r in range(1, parts.shape[0]):
        total = total + parts[r].astype(F32)
    d_input[...] = (up_own[...].astype(F32) + total[:, :width]).astype(BF16)
    for i in range(width // 128):
        grad_gain[:, i * 128 : (i + 1) * 128] = total[i : i + 1, width:]


def per_device(
    act_log, grad_log, failed_section, live_tokens, gate_weight, up_weight, down_weight, norm_gain
):
    ny, nzh, nx = (lax.axis_size(a) for a in ROWS_AXES)
    nzl, nc = lax.axis_size("zl"), lax.axis_size("c")
    sections = ny * nzh
    shards = sections * nx
    tokens, width = act_log.shape[1:]
    batches = live_tokens.shape[0]
    rows = batches * tokens
    live = 3 * rows // 4
    per = tokens // (ny * nx)
    cycles = live // tokens
    features = float(width * nzl * nc)
    hid = gate_weight.shape[1]
    failed = failed_section[0]
    source = (failed + sections - 1) % sections
    target = (failed + 1) % sections
    batch = jnp.arange(batches, dtype=jnp.int32)
    offs = jnp.sum(jnp.where(batch[None, :] < batch[:, None], live_tokens[None, :], 0), axis=1)
    x = lax.axis_index("x")
    me = lax.axis_index(ROWS_AXES)
    plan = (batches, tokens, per, nx, cycles * per, ny * cycles * per)

    def shape(*dims, dtype=BF16):
        return jax.ShapeDtypeStruct(dims, dtype)

    nums = jnp.stack([lax.axis_index("c"), x, me, lax.axis_index("zl")]).astype(jnp.int32)
    nums = jnp.concatenate([nums, live_tokens, offs.astype(jnp.int32)])
    send = call(
        functools.partial(scatter_kernel, per), shape(2 * tokens, width),
        [
            pltpu.VMEM((tokens, width), BF16),
            pltpu.VMEM((tokens, width), BF16),
            pltpu.SemaphoreType.DMA((2, COPIES)),
        ],
        4 * tokens * tokens * width, live_tokens, act_log, grad_log, away=(1, 2),
    )
    recv = lax.all_to_all(send, ("y", "x"), 0, 0, tiled=True).reshape(ny * nx, 2 * per, width)
    got = jnp.stack(
        [
            lax.dynamic_slice_in_dim(recv, source // nzh * nx, nx, 0)[:, :per],
            lax.dynamic_slice_in_dim(recv, target // nzh * nx, nx, 0)[:, per:],
        ]
    )
    place = lax.axis_index(("y", "x")) * per + jnp.arange(per, dtype=jnp.int32)
    slot = (place[None, :] - offs[:, None]) % tokens
    cycle = (offs[:, None] + slot) // tokens
    hit = (slot < live_tokens[:, None])[:, None, :] & (
        cycle[:, None, :] == jnp.arange(cycles, dtype=jnp.int32)[None, :, None]
    )
    packed = jnp.sum(
        jnp.where(hit[None, :, :, :, None], got[:, :, None].astype(F32), 0.0), axis=1
    ).astype(BF16)
    block = cycles * per
    packed = packed.reshape(2 * block, width)

    other = lax.ppermute(packed, "zh", [(0, 1), (1, 0)])
    packed = jnp.where(lax.axis_index("zh") == source % nzh, packed, other)

    copies = jnp.broadcast_to(packed[None], (ny,) + packed.shape).reshape(-1, width)
    column = lax.all_to_all(copies, "y", 0, 0, tiled=True)
    part = ny * block
    out_row = lax.broadcasted_iota(jnp.int32, (2 * part, 2 * part), 0)
    from_row = lax.broadcasted_iota(jnp.int32, (2 * part, 2 * part), 1)
    at = out_row % part
    hot = (at // block * 2 + out_row // part) * block + at % block == from_row
    own = contract(hot.astype(BF16), column, 1, 0).astype(BF16).reshape(2, part, width)
    forth = [(i, (i + 1) % nx) for i in range(nx)]
    back = [(i, (i - 1) % nx) for i in range(nx)]
    right = lax.ppermute(own, "x", forth)
    left = lax.ppermute(own, "x", back)
    over_in = lax.ppermute(right[0], "x", forth)
    over_up = lax.ppermute(left[1], "x", back)
    blocks = (own, right, left, over_in, over_up)

    inside = width - 2 * hid
    gate_rows, up_rows = gate_weight.T, up_weight.T
    ahead_rows = jnp.concatenate([gate_rows, up_rows, jnp.zeros((inside, width), BF16)], axis=0)
    behind_rows = jnp.concatenate([jnp.zeros((2 * hid, width), BF16), down_weight[:inside]], axis=0)
    rest_rows = down_weight[inside:]
    gain = norm_gain.reshape(1, width)
    own_count = live // nc // nzl
    size = own_count * (width // 128) + TAIL
    product = 2 * live * width * WIDE
    halves = shape(nzl, size, 128)
    keep, give = call(
        terms_kernel, (halves, halves), [pltpu.VMEM((live, 128), F32)], 5 * product,
        nums, *blocks, gain, ahead_rows, behind_rows, rest_rows,
    )
    taken = lax.ppermute(give, "c", [(0, 1), (1, 0)])
    chunk = shape(size, 128)
    pairs = call(pair_kernel, (chunk,) * nzl, [], nzl * size * 128, nums, keep, taken)
    others = [
        lax.ppermute(pairs[i], "zl", [(a, (a + i) % nzl) for a in range(nzl)]) for i in range(1, nzl)
    ]
    point = call(
        functools.partial(point_kernel, hid, features), chunk,
        [
            pltpu.VMEM((own_count, width), F32),
            pltpu.VMEM((own_count, hid), F32),
            pltpu.VMEM((128, 128), F32),
        ],
        20 * size * 128, pairs[0], *others,
    )
    every = lax.all_gather(point, ("zl", "c"), axis=0, tiled=True)

    own_rows = rows // shards
    count = rows // nx
    out, up_own = call(
        functools.partial(term_kernel, hid, features, plan),
        (shape(nx, count + 16, width), shape(own_rows, width)),
        [pltpu.VMEM((live, width), BF16), pltpu.VMEM((3, live, WIDE), BF16)],
        5 * product,
        nums, *blocks, every, gain, gate_rows, up_rows,
    )
    out = lax.all_to_all(out, "x", 0, 0, tiled=True)
    out = call(
        middle_kernel, shape(sections, own_rows, width + 128), [], nx * count * width, out
    )
    out = lax.all_to_all(out, ("y", "zh"), 0, 0, tiled=True)
    d_input, grad_gain = call(
        final_kernel, (shape(own_rows, width), shape(1, width, dtype=F32)), [],
        sections * own_rows * width, out, up_own,
    )

    grad_gate, grad_up, grad_down = call(
        functools.partial(grads_kernel, hid),
        (shape(hid, width),) * 3,
        [
            pltpu.VMEM((3, live, WIDE), BF16),
            pltpu.VMEM((live, width), BF16),
            pltpu.VMEM((live, width), BF16),
        ],
        3 * product,
        *blocks, every, gain,
    )
    return (d_input, grad_gate.T, grad_up.T, grad_down, grad_gain.reshape(width))


def solution(mesh):
    fine = Mesh(mesh.devices.reshape(8, 2, 4, 4, 2), AXES)
    section, replica, tensor = ("y", "zh"), "x", ("zl", "c")
    split = ("y", "zh", "x")
    in_specs = (
        P(section, replica, tensor),
        P(section, replica, tensor),
        P(),
        P(),
        P(tensor, split),
        P(tensor, split),
        P(split, tensor),
        P(tensor),
    )
    out_specs = (
        P(split, tensor),
        P(tensor, split),
        P(tensor, split),
        P(split, tensor),
        P(tensor),
    )
    return jax.shard_map(
        per_device, mesh=fine, in_specs=in_specs, out_specs=out_specs, check_vma=False
    )
```

```python
import functools

import jax
import jax.numpy as jnp
from jax import lax
from jax.experimental import pallas as pl
from jax.experimental.pallas import tpu as pltpu
from jax.sharding import Mesh, PartitionSpec as P

AXES = ("y", "zh", "x", "zl", "c")
ROWS_AXES = ("y", "zh", "x")
F32 = jnp.float32
BF16 = jnp.bfloat16
WIDE = 256
VMEM = pl.BlockSpec(memory_space=pltpu.VMEM)
SMEM = pl.BlockSpec(memory_space=pltpu.SMEM)


def contract(left, right, l, r):
    return lax.dot_general(left, right, (((l,), (r,)), ((), ())), preferred_element_type=F32)


def call(body, outs, scratch, flops, *args):
    moved = sum(a.size * a.dtype.itemsize for a in args) + sum(
        o.size * o.dtype.itemsize for o in jax.tree.leaves(outs)
    )
    return pl.pallas_call(
        body,
        out_shape=outs,
        in_specs=[
            SMEM if a.ndim == 1 else VMEM for a in args
        ],
        out_specs=jax.tree.map(lambda _: VMEM, outs),
        scratch_shapes=scratch,
        compiler_params=pltpu.CompilerParams(vmem_limit_bytes=48 * 1024 * 1024),
        cost_estimate=pl.CostEstimate(flops=flops, bytes_accessed=moved, transcendentals=0),
    )(*args)


def pick(refs, k):
    own, right, left, over_in, over_up = refs
    if k < 3:
        ref = (own, right, left)[k]
        return ref[0], ref[1]
    return over_in[...], over_up[...]


def log2(n):
    assert n & (n - 1) == 0
    return n.bit_length() - 1


CORE, REPLICA, ME, LINE, LIVE = 0, 1, 2, 3, 4


def scatter_kernel(per, live, act, grad, send):
    tokens, width = act.shape[1:]
    x = lax.axis_index("x")
    off = jnp.int32(0)
    for b in range(live.shape[0] - 1):
        off = off + jnp.where(x > b, live[b], 0)
    row = lax.broadcasted_iota(jnp.int32, (tokens, tokens), 0)
    column = lax.broadcasted_iota(jnp.int32, (tokens, tokens), 1)
    roll = ((row - column - off) & (tokens - 1)) == 0
    roll = jnp.where(roll, 1.0, 0.0).astype(BF16)
    groups = (tokens // per, per, width)
    first = contract(roll, act[0], 1, 0).reshape(groups)
    second = contract(roll, grad[0], 1, 0).reshape(groups)
    send[...] = jnp.concatenate([first, second], axis=1).reshape(2 * tokens, width).astype(BF16)


TAIL = 16


def terms_of(inputs, upstream, gain, ahead, behind, rest, tail_ref):
    gain_wide = gain[...].astype(F32)
    n = inputs.shape[0]
    chunk = n // 2
    extra = rest.shape[0]
    wide = inputs.astype(F32)
    scaled = (wide * gain_wide).astype(BF16)
    main = contract(scaled, ahead[...], 1, 1) + contract(upstream, behind[...], 1, 1)
    main = main.astype(BF16)
    squares = jnp.sum(wide * wide, axis=1, keepdims=True)
    high = squares.astype(BF16).astype(F32)
    tail_ref[...] = jnp.zeros(tail_ref.shape, F32)
    tail_ref[:, :extra] = contract(upstream, rest[...], 1, 1)
    tail_ref[:, extra : extra + 1] = high
    tail_ref[:, extra + 1 : extra + 2] = squares - high
    tails = [tail_ref[h * chunk : (h + 1) * chunk, :].T[:TAIL].astype(BF16) for h in range(2)]

    def store(out):
        for h in range(2):
            for i in range(main.shape[1] // 128):
                out[h, i * chunk : (i + 1) * chunk, :] = main[
                    h * chunk : (h + 1) * chunk, i * 128 : (i + 1) * 128
                ]
            out[h, -TAIL:, :] = jnp.zeros((TAIL, 128), BF16)
            out[h, -TAIL:, :chunk] = tails[h]

    return store


def by_core(nums, store, first, second):
    pl.when(nums[CORE] == 0)(functools.partial(store, first))
    pl.when(nums[CORE] != 0)(functools.partial(store, second))


def early_kernel(nums, own, right, left, gain, ahead, behind, rest, keep, send, middle, *tail_refs):
    weights = (gain, ahead, behind, rest)
    by_core(nums, terms_of(own[0], own[1], *weights, tail_refs[0]), keep, send)
    by_core(nums, terms_of(left[0], left[1], *weights, tail_refs[1]), send, keep)
    terms_of(right[0], right[1], *weights, tail_refs[2])(middle)


def late_kernel(nums, middle, over_in, over_up, gain, ahead, behind, rest, keep, send, tail_ref):
    def passed(out):
        out[...] = middle[...]

    by_core(nums, passed, keep, send)
    store = terms_of(over_in[...], over_up[...], gain, ahead, behind, rest, tail_ref)
    by_core(nums, store, send, keep)


def pair_kernel(nums, keep_a, keep_b, recv_a, recv_b, *outs):
    for i, out in enumerate(outs):
        chunk = (nums[LINE] + i) & (len(outs) - 1)

        def add(keep, recv, out=out, at=chunk & 1):
            out[...] = (keep[at].astype(F32) + recv[at].astype(F32)).astype(BF16)

        pl.when(chunk < 2)(functools.partial(add, keep_a, recv_a))
        pl.when(chunk >= 2)(functools.partial(add, keep_b, recv_b))


def point_kernel(hid, features, *refs):
    terms, (out, main_ref, hg_ref, tail_ref) = refs[:-4], refs[-4:]
    rows, width = main_ref.shape
    total = terms[0][...].astype(F32)
    for t in terms[1:]:
        total = total + t[...].astype(F32)
    for i in range(width // 128):
        main_ref[:, i * 128 : (i + 1) * 128] = total[i * rows : (i + 1) * rows]
    tail = total[-TAIL:].T[:rows]
    inside = width - 2 * hid
    gate = main_ref[:, :hid]
    up = main_ref[:, hid : 2 * hid]
    hg_ref[:, :inside] = main_ref[:, 2 * hid :]
    hg_ref[:, inside:] = tail[:, : hid - inside]
    hidden_grad = hg_ref[...]
    squares = tail[:, hid - inside : hid - inside + 1] + tail[:, hid - inside + 1 : hid - inside + 2]
    inv_rms = lax.rsqrt(squares / features + 1e-05)
    gate = gate * inv_rms
    up = up * inv_rms
    logistic = jax.nn.sigmoid(gate)
    swished = gate * logistic
    slopes = logistic * (1.0 + gate * (1.0 - logistic))
    d_gate = (hidden_grad * up * slopes).astype(BF16).astype(F32)
    d_up = (hidden_grad * swished).astype(BF16).astype(F32)
    inner = jnp.sum(d_gate * gate + d_up * up, axis=1, keepdims=True)
    main_ref[:, :hid] = swished * up
    main_ref[:, hid : 2 * hid] = d_gate
    main_ref[:, 2 * hid :] = d_up[:, :inside]
    inv_hi = inv_rms.astype(BF16).astype(F32)
    in_hi = inner.astype(BF16).astype(F32)
    tail_ref[...] = jnp.zeros(tail_ref.shape, F32)
    tail_ref[:rows, : hid - inside] = d_up[:, inside:]
    for i, v in enumerate((inv_hi, inv_rms - inv_hi, in_hi, inner - in_hi)):
        at = hid - inside + i
        tail_ref[:rows, at : at + 1] = v
    for i in range(width // 128):
        out[i * rows : (i + 1) * rows, :] = main_ref[:, i * 128 : (i + 1) * 128].astype(BF16)
    out[-TAIL:, :] = tail_ref[...].T[:TAIL].astype(BF16)


def rows_of(every, k, n, hid, width, pay_ref):
    own = n // 2
    pieces = width // 128
    size = pieces * own + TAIL
    inside = width - 2 * hid
    tails = []
    for j in range(2):
        at = (((k % 2) * 2 + j) * 2 + k // 2) * size
        r = slice(k * n + j * own, k * n + (j + 1) * own)
        main = jnp.concatenate(
            [every[at + i * own : at + (i + 1) * own, :] for i in range(pieces)], axis=1
        )
        tail = every[at + pieces * own : at + size, :].astype(F32).T[:own]
        pay_ref[0, r, :hid] = main[:, :hid]
        pay_ref[1, r, :hid] = main[:, hid : 2 * hid]
        pay_ref[2, r, :inside] = main[:, 2 * hid :]
        pay_ref[2, r, inside:hid] = tail[:, : hid - inside].astype(BF16)
        tails.append(tail[:, hid - inside :])
    tail = jnp.concatenate(tails, axis=0)
    return tail[:, 0:1] + tail[:, 1:2], tail[:, 2:3] + tail[:, 3:4]


def where_packed(nums, row, batches, tokens, per, nx, block, part):
    batch = row >> log2(tokens)
    slot = row & (tokens - 1)
    limit, off = jnp.zeros_like(row), jnp.zeros_like(row)
    for b in range(batches):
        limit = jnp.where(batch == b, nums[LIVE + b], limit)
        off = jnp.where(batch == b, nums[LIVE + batches + b], off)
    at = off + slot
    device = (at & (tokens - 1)) >> log2(per)
    turn = (device - nums[REPLICA] + nx) & (nx - 1)
    held = jnp.where(turn == nx - 1, 1, jnp.where(turn == 1, 2, jnp.where(turn == 2, 3, 0)))
    index = held * part + (device >> log2(nx)) * block + (at >> log2(tokens)) * per + (at & (per - 1))
    return jnp.where(slot < limit, index, -1)


def term_kernel(
    hid, features, plan, nums, own, right, left, over_in, over_up, every, gain, gate, up,
    out, up_own, term_ref, pay_ref,
):
    nx = out.shape[0]
    gain_wide = gain[...].astype(F32)
    gain_term = jnp.zeros(gain_wide.shape, F32)
    own_rows = up_own.shape[0]
    own_total = jnp.zeros(up_own.shape, F32)
    row = nums[ME] * own_rows + lax.broadcasted_iota(jnp.int32, (own_rows, 1), 0)
    index = where_packed(nums, row, *plan)
    for k in range(4):
        inputs, upstream = pick((own, right, left, over_in, over_up), k)
        n = inputs.shape[0]
        s = slice(k * n, (k + 1) * n)
        inv_rms, inner = rows_of(every, k, n, hid, inputs.shape[1], pay_ref)
        d_normed = contract(pay_ref[1, s, :hid], gate[...], 1, 0) + contract(
            pay_ref[2, s, :hid], up[...], 1, 0
        )
        unit = inputs.astype(F32) * inv_rms
        gain_term = gain_term + jnp.sum(d_normed * unit, axis=0, keepdims=True)
        term = inv_rms * (gain_wide * d_normed - unit * (inner / features))
        term_ref[s, :] = term.astype(BF16)
        column = lax.broadcasted_iota(jnp.int32, (own_rows, n), 1) + k * n
        hot = jnp.where(index == column, 1.0, 0.0).astype(BF16)
        own_total = own_total + contract(hot, upstream, 1, 0)
    up_own[...] = own_total.astype(BF16)
    gain_hi = gain_term.astype(BF16).astype(F32)
    rows = plan[0] * plan[1] // nx
    extra = out.shape[1] - rows
    row = lax.broadcasted_iota(jnp.int32, (extra, gain_term.shape[1]), 0)
    extras = jnp.where(row == 0, gain_hi, jnp.where(row == 1, gain_term - gain_hi, 0.0)).astype(BF16)
    live = term_ref.shape[0]
    column = lax.broadcasted_iota(jnp.int32, (rows, live), 1)
    i = lax.broadcasted_iota(jnp.int32, (rows, 1), 0)
    for q in range(nx):
        row = (((i >> log2(own_rows)) * nx + q) << log2(own_rows)) + (i & (own_rows - 1))
        hot = jnp.where(where_packed(nums, row, *plan) == column, 1.0, 0.0).astype(BF16)
        out[q, :rows, :] = contract(hot, term_ref[...], 1, 0).astype(BF16)
        out[q, rows:, :] = extras


def grads_kernel(
    hid, own, right, left, over_in, over_up, every, gain,
    grad_gate, grad_up, grad_down, pay_ref, normed_ref, up_ref,
):
    gain_wide = gain[...].astype(F32)
    for k in range(4):
        inputs, upstream = pick((own, right, left, over_in, over_up), k)
        n = inputs.shape[0]
        s = slice(k * n, (k + 1) * n)
        inv_rms, _ = rows_of(every, k, n, hid, inputs.shape[1], pay_ref)
        normed_ref[s, :] = (inputs.astype(F32) * inv_rms * gain_wide).astype(BF16)
        up_ref[s, :] = upstream
    grad_down[...] = contract(pay_ref[0, :, :hid], up_ref[...], 0, 0).astype(BF16)
    normed = normed_ref[...]
    grad_gate[...] = contract(pay_ref[1, :, :hid], normed, 0, 0).astype(BF16)
    grad_up[...] = contract(pay_ref[2, :, :hid], normed, 0, 0).astype(BF16)


def middle_kernel(parts, out):
    sections, own_rows, lanes = out.shape
    width = parts.shape[2]
    rows = sections * own_rows
    total = parts[0].astype(F32)
    for r in range(1, parts.shape[0]):
        total = total + parts[r].astype(F32)
    out[:, :, :width] = total[:rows].astype(BF16).reshape(sections, own_rows, width)
    gain = total[rows : rows + 1] + total[rows + 1 : rows + 2]
    row = lax.broadcasted_iota(jnp.int32, (own_rows, 128), 0)
    tile = jnp.zeros((own_rows, 128), F32)
    for i in range(width // 128):
        tile = jnp.where(row == i, gain[:, i * 128 : (i + 1) * 128], tile)
    tile = tile.astype(BF16)
    for s in range(sections):
        out[s, :, width:] = tile


def final_kernel(parts, up_own, d_input, grad_gain):
    width = up_own.shape[1]
    total = parts[0].astype(F32)
    for r in range(1, parts.shape[0]):
        total = total + parts[r].astype(F32)
    d_input[...] = (up_own[...].astype(F32) + total[:, :width]).astype(BF16)
    for i in range(width // 128):
        grad_gain[:, i * 128 : (i + 1) * 128] = total[i : i + 1, width:]


def per_device(
    act_log, grad_log, failed_section, live_tokens, gate_weight, up_weight, down_weight, norm_gain
):
    ny, nzh, nx = (lax.axis_size(a) for a in ROWS_AXES)
    nzl, nc = lax.axis_size("zl"), lax.axis_size("c")
    sections = ny * nzh
    shards = sections * nx
    tokens, width = act_log.shape[1:]
    batches = live_tokens.shape[0]
    rows = batches * tokens
    live = 3 * rows // 4
    per = tokens // (ny * nx)
    cycles = live // tokens
    features = float(width * nzl * nc)
    hid = gate_weight.shape[1]
    failed = failed_section[0]
    source = (failed + sections - 1) % sections
    target = (failed + 1) % sections
    batch = jnp.arange(batches, dtype=jnp.int32)
    offs = jnp.sum(jnp.where(batch[None, :] < batch[:, None], live_tokens[None, :], 0), axis=1)
    x = lax.axis_index("x")
    me = lax.axis_index(ROWS_AXES)
    plan = (batches, tokens, per, nx, cycles * per, ny * cycles * per)

    def shape(*dims, dtype=BF16):
        return jax.ShapeDtypeStruct(dims, dtype)

    nums = jnp.stack([lax.axis_index("c"), x, me, lax.axis_index("zl")]).astype(jnp.int32)
    nums = jnp.concatenate([nums, live_tokens, offs.astype(jnp.int32)])
    send = call(
        functools.partial(scatter_kernel, per), shape(2 * tokens, width), [],
        4 * tokens * tokens * width, live_tokens, act_log, grad_log,
    )
    recv = lax.all_to_all(send, ("y", "x"), 0, 0, tiled=True).reshape(ny * nx, 2 * per, width)
    got = jnp.stack(
        [
            lax.dynamic_slice_in_dim(recv, source // nzh * nx, nx, 0)[:, :per],
            lax.dynamic_slice_in_dim(recv, target // nzh * nx, nx, 0)[:, per:],
        ]
    )
    place = lax.axis_index(("y", "x")) * per + jnp.arange(per, dtype=jnp.int32)
    slot = (place[None, :] - offs[:, None]) % tokens
    cycle = (offs[:, None] + slot) // tokens
    hit = (slot < live_tokens[:, None])[:, None, :] & (
        cycle[:, None, :] == jnp.arange(cycles, dtype=jnp.int32)[None, :, None]
    )
    packed = jnp.sum(
        jnp.where(hit[None, :, :, :, None], got[:, :, None].astype(F32), 0.0), axis=1
    ).astype(BF16)
    block = cycles * per
    packed = packed.reshape(2 * block, width)

    other = lax.ppermute(packed, "zh", [(0, 1), (1, 0)])
    packed = jnp.where(lax.axis_index("zh") == source % nzh, packed, other)

    copies = jnp.broadcast_to(packed[None], (ny,) + packed.shape).reshape(-1, width)
    column = lax.all_to_all(copies, "y", 0, 0, tiled=True)
    part = ny * block
    out_row = lax.broadcasted_iota(jnp.int32, (2 * part, 2 * part), 0)
    from_row = lax.broadcasted_iota(jnp.int32, (2 * part, 2 * part), 1)
    at = out_row % part
    hot = (at // block * 2 + out_row // part) * block + at % block == from_row
    own = contract(hot.astype(BF16), column, 1, 0).astype(BF16).reshape(2, part, width)
    forth = [(i, (i + 1) % nx) for i in range(nx)]
    back = [(i, (i - 1) % nx) for i in range(nx)]
    right = lax.ppermute(own, "x", forth)
    left = lax.ppermute(own, "x", back)
    over_in = lax.ppermute(right[0], "x", forth)
    over_up = lax.ppermute(left[1], "x", back)
    blocks = (own, right, left, over_in, over_up)

    inside = width - 2 * hid
    gate_rows, up_rows = gate_weight.T, up_weight.T
    ahead_rows = jnp.concatenate([gate_rows, up_rows, jnp.zeros((inside, width), BF16)], axis=0)
    behind_rows = jnp.concatenate([jnp.zeros((2 * hid, width), BF16), down_weight[:inside]], axis=0)
    rest_rows = down_weight[inside:]
    gain = norm_gain.reshape(1, width)
    own_count = live // nc // nzl
    size = own_count * (width // 128) + TAIL
    product = 2 * live * width * WIDE
    two = shape(2, size, 128)
    weights = (gain, ahead_rows, behind_rows, rest_rows)
    tail_ref = pltpu.VMEM((part, 128), F32)
    swap = [(0, 1), (1, 0)]
    keep_a, give_a, middle = call(
        early_kernel, (two,) * 3, [tail_ref] * 3, 4 * product, nums, own, right, left, *weights
    )
    taken_a = lax.ppermute(give_a, "c", swap)
    keep_b, give_b = call(
        late_kernel, (two,) * 2, [tail_ref], product, nums, middle, over_in, over_up, *weights
    )
    taken_b = lax.ppermute(give_b, "c", swap)
    chunk = shape(size, 128)
    pairs = call(pair_kernel, (chunk,) * nzl, [], nzl * size * 128, nums, keep_a, keep_b, taken_a, taken_b)
    others = [
        lax.ppermute(pairs[i], "zl", [(a, (a + i) % nzl) for a in range(nzl)]) for i in range(1, nzl)
    ]
    point = call(
        functools.partial(point_kernel, hid, features), chunk,
        [
            pltpu.VMEM((own_count, width), F32),
            pltpu.VMEM((own_count, hid), F32),
            pltpu.VMEM((128, 128), F32),
        ],
        20 * size * 128, pairs[0], *others,
    )
    every = lax.all_gather(point, ("zl", "c"), axis=0, tiled=True)

    own_rows = rows // shards
    count = rows // nx
    out, up_own = call(
        functools.partial(term_kernel, hid, features, plan),
        (shape(nx, count + 16, width), shape(own_rows, width)),
        [pltpu.VMEM((live, width), BF16), pltpu.VMEM((3, live, WIDE), BF16)],
        5 * product,
        nums, *blocks, every, gain, gate_rows, up_rows,
    )
    out = lax.all_to_all(out, "x", 0, 0, tiled=True)
    out = call(
        middle_kernel, shape(sections, own_rows, width + 128), [], nx * count * width, out
    )
    out = lax.all_to_all(out, ("y", "zh"), 0, 0, tiled=True)
    d_input, grad_gain = call(
        final_kernel, (shape(own_rows, width), shape(1, width, dtype=F32)), [],
        sections * own_rows * width, out, up_own,
    )

    grad_gate, grad_up, grad_down = call(
        functools.partial(grads_kernel, hid),
        (shape(hid, width),) * 3,
        [
            pltpu.VMEM((3, live, WIDE), BF16),
            pltpu.VMEM((live, width), BF16),
            pltpu.VMEM((live, width), BF16),
        ],
        3 * product,
        *blocks, every, gain,
    )
    return (d_input, grad_gate.T, grad_up.T, grad_down, grad_gain.reshape(width))


def solution(mesh):
    fine = Mesh(mesh.devices.reshape(8, 2, 4, 4, 2), AXES)
    section, replica, tensor = ("y", "zh"), "x", ("zl", "c")
    split = ("y", "zh", "x")
    in_specs = (
        P(section, replica, tensor),
        P(section, replica, tensor),
        P(),
        P(),
        P(tensor, split),
        P(tensor, split),
        P(split, tensor),
        P(tensor),
    )
    out_specs = (
        P(split, tensor),
        P(tensor, split),
        P(tensor, split),
        P(split, tensor),
        P(tensor),
    )
    return jax.shard_map(
        per_device, mesh=fine, in_specs=in_specs, out_specs=out_specs, check_vma=False
    )
```

```python
import functools

import jax
import jax.numpy as jnp
from jax import lax
from jax.experimental import pallas as pl
from jax.experimental.pallas import tpu as pltpu
from jax.sharding import Mesh, PartitionSpec as P

AXES = ("y", "zh", "x", "zl", "c")
ROWS_AXES = ("y", "zh", "x")
F32 = jnp.float32
BF16 = jnp.bfloat16
WIDE = 256
VMEM = pl.BlockSpec(memory_space=pltpu.VMEM)
SMEM = pl.BlockSpec(memory_space=pltpu.SMEM)


def contract(left, right, l, r):
    return lax.dot_general(left, right, (((l,), (r,)), ((), ())), preferred_element_type=F32)


def call(body, outs, scratch, flops, *args):
    moved = sum(a.size * a.dtype.itemsize for a in args) + sum(
        o.size * o.dtype.itemsize for o in jax.tree.leaves(outs)
    )
    return pl.pallas_call(
        body,
        out_shape=outs,
        in_specs=[
            SMEM if a.ndim == 1 else VMEM for a in args
        ],
        out_specs=jax.tree.map(lambda _: VMEM, outs),
        scratch_shapes=scratch,
        compiler_params=pltpu.CompilerParams(vmem_limit_bytes=48 * 1024 * 1024),
        cost_estimate=pl.CostEstimate(flops=flops, bytes_accessed=moved, transcendentals=0),
    )(*args)


def pick(refs, k):
    own, right, left, over_in, over_up = refs
    if k < 3:
        ref = (own, right, left)[k]
        return ref[0], ref[1]
    return over_in[...], over_up[...]


def log2(n):
    assert n & (n - 1) == 0
    return n.bit_length() - 1


CORE, REPLICA, ME, LINE, LIVE = 0, 1, 2, 3, 4


def scatter_kernel(per, live, act, grad, send):
    tokens, width = act.shape[1:]
    x = lax.axis_index("x")
    off = jnp.int32(0)
    for b in range(live.shape[0] - 1):
        off = off + jnp.where(x > b, live[b], 0)
    row = lax.broadcasted_iota(jnp.int32, (tokens, tokens), 0)
    column = lax.broadcasted_iota(jnp.int32, (tokens, tokens), 1)
    roll = ((row - column - off) & (tokens - 1)) == 0
    roll = jnp.where(roll, 1.0, 0.0).astype(BF16)
    groups = (tokens // per, per, width)
    first = contract(roll, act[0], 1, 0).reshape(groups)
    second = contract(roll, grad[0], 1, 0).reshape(groups)
    send[...] = jnp.concatenate([first, second], axis=1).reshape(2 * tokens, width).astype(BF16)


TAIL = 16


def terms_of(inputs, upstream, gain, ahead, behind, rest, tail_ref):
    gain_wide = gain[...].astype(F32)
    n = inputs.shape[0]
    chunk = n // 2
    extra = rest.shape[0]
    wide = inputs.astype(F32)
    scaled = (wide * gain_wide).astype(BF16)
    main = contract(scaled, ahead[...], 1, 1) + contract(upstream, behind[...], 1, 1)
    main = main.astype(BF16)
    squares = jnp.sum(wide * wide, axis=1, keepdims=True)
    high = squares.astype(BF16).astype(F32)
    tail_ref[...] = jnp.zeros(tail_ref.shape, F32)
    tail_ref[:, :extra] = contract(upstream, rest[...], 1, 1)
    tail_ref[:, extra : extra + 1] = high
    tail_ref[:, extra + 1 : extra + 2] = squares - high
    tails = [tail_ref[h * chunk : (h + 1) * chunk, :].T[:TAIL].astype(BF16) for h in range(2)]

    def store(out):
        for h in range(2):
            for i in range(main.shape[1] // 128):
                out[h, i * chunk : (i + 1) * chunk, :] = main[
                    h * chunk : (h + 1) * chunk, i * 128 : (i + 1) * 128
                ]
            out[h, -TAIL:, :] = jnp.zeros((TAIL, 128), BF16)
            out[h, -TAIL:, :chunk] = tails[h]

    return store


def by_core(nums, store, first, second):
    pl.when(nums[CORE] == 0)(functools.partial(store, first))
    pl.when(nums[CORE] != 0)(functools.partial(store, second))


def early_kernel(nums, own, right, left, gain, ahead, behind, rest, keep, send, middle, *tail_refs):
    weights = (gain, ahead, behind, rest)
    by_core(nums, terms_of(own[0], own[1], *weights, tail_refs[0]), keep, send)
    by_core(nums, terms_of(left[0], left[1], *weights, tail_refs[1]), send, keep)
    terms_of(right[0], right[1], *weights, tail_refs[2])(middle)


def late_kernel(nums, middle, over_in, over_up, gain, ahead, behind, rest, keep, send, tail_ref):
    def passed(out):
        out[...] = middle[...]

    by_core(nums, passed, keep, send)
    store = terms_of(over_in[...], over_up[...], gain, ahead, behind, rest, tail_ref)
    by_core(nums, store, send, keep)


def pair_kernel(nums, keep_a, keep_b, recv_a, recv_b, *outs):
    for i, out in enumerate(outs):
        chunk = nums[LINE] ^ i

        def add(keep, recv, out=out, at=chunk & 1):
            out[...] = (keep[at].astype(F32) + recv[at].astype(F32)).astype(BF16)

        pl.when(chunk < 2)(functools.partial(add, keep_a, recv_a))
        pl.when(chunk >= 2)(functools.partial(add, keep_b, recv_b))


def point_kernel(hid, features, *refs):
    terms, (out, main_ref, hg_ref, tail_ref) = refs[:-4], refs[-4:]
    rows, width = main_ref.shape
    total = terms[0][...].astype(F32)
    for t in terms[1:]:
        total = total + t[...].astype(F32)
    for i in range(width // 128):
        main_ref[:, i * 128 : (i + 1) * 128] = total[i * rows : (i + 1) * rows]
    tail = total[-TAIL:].T[:rows]
    inside = width - 2 * hid
    gate = main_ref[:, :hid]
    up = main_ref[:, hid : 2 * hid]
    hg_ref[:, :inside] = main_ref[:, 2 * hid :]
    hg_ref[:, inside:] = tail[:, : hid - inside]
    hidden_grad = hg_ref[...]
    squares = tail[:, hid - inside : hid - inside + 1] + tail[:, hid - inside + 1 : hid - inside + 2]
    inv_rms = lax.rsqrt(squares / features + 1e-05)
    gate = gate * inv_rms
    up = up * inv_rms
    logistic = jax.nn.sigmoid(gate)
    swished = gate * logistic
    slopes = logistic * (1.0 + gate * (1.0 - logistic))
    d_gate = (hidden_grad * up * slopes).astype(BF16).astype(F32)
    d_up = (hidden_grad * swished).astype(BF16).astype(F32)
    inner = jnp.sum(d_gate * gate + d_up * up, axis=1, keepdims=True)
    main_ref[:, :hid] = swished * up
    main_ref[:, hid : 2 * hid] = d_gate
    main_ref[:, 2 * hid :] = d_up[:, :inside]
    inv_hi = inv_rms.astype(BF16).astype(F32)
    in_hi = inner.astype(BF16).astype(F32)
    tail_ref[...] = jnp.zeros(tail_ref.shape, F32)
    tail_ref[:rows, : hid - inside] = d_up[:, inside:]
    for i, v in enumerate((inv_hi, inv_rms - inv_hi, in_hi, inner - in_hi)):
        at = hid - inside + i
        tail_ref[:rows, at : at + 1] = v
    for i in range(width // 128):
        out[i * rows : (i + 1) * rows, :] = main_ref[:, i * 128 : (i + 1) * 128].astype(BF16)
    out[-TAIL:, :] = tail_ref[...].T[:TAIL].astype(BF16)


def rows_of(every, k, n, hid, width, pay_ref):
    own = n // 2
    pieces = width // 128
    size = pieces * own + TAIL
    inside = width - 2 * hid
    tails = []
    for j in range(2):
        at = (((k % 2) * 2 + j) * 2 + k // 2) * size
        r = slice(k * n + j * own, k * n + (j + 1) * own)
        main = jnp.concatenate(
            [every[at + i * own : at + (i + 1) * own, :] for i in range(pieces)], axis=1
        )
        tail = every[at + pieces * own : at + size, :].astype(F32).T[:own]
        pay_ref[0, r, :hid] = main[:, :hid]
        pay_ref[1, r, :hid] = main[:, hid : 2 * hid]
        pay_ref[2, r, :inside] = main[:, 2 * hid :]
        pay_ref[2, r, inside:hid] = tail[:, : hid - inside].astype(BF16)
        tails.append(tail[:, hid - inside :])
    tail = jnp.concatenate(tails, axis=0)
    return tail[:, 0:1] + tail[:, 1:2], tail[:, 2:3] + tail[:, 3:4]


def where_packed(nums, row, batches, tokens, per, nx, block, part):
    batch = row >> log2(tokens)
    slot = row & (tokens - 1)
    limit, off = jnp.zeros_like(row), jnp.zeros_like(row)
    for b in range(batches):
        limit = jnp.where(batch == b, nums[LIVE + b], limit)
        off = jnp.where(batch == b, nums[LIVE + batches + b], off)
    at = off + slot
    device = (at & (tokens - 1)) >> log2(per)
    turn = (device - nums[REPLICA] + nx) & (nx - 1)
    held = jnp.where(turn == nx - 1, 1, jnp.where(turn == 1, 2, jnp.where(turn == 2, 3, 0)))
    index = held * part + (device >> log2(nx)) * block + (at >> log2(tokens)) * per + (at & (per - 1))
    return jnp.where(slot < limit, index, -1)


def term_kernel(
    hid, features, plan, nums, own, right, left, over_in, over_up, every, gain, gate, up,
    out, up_own, term_ref, pay_ref,
):
    nx = out.shape[0]
    gain_wide = gain[...].astype(F32)
    gain_term = jnp.zeros(gain_wide.shape, F32)
    own_rows = up_own.shape[0]
    own_total = jnp.zeros(up_own.shape, F32)
    row = nums[ME] * own_rows + lax.broadcasted_iota(jnp.int32, (own_rows, 1), 0)
    index = where_packed(nums, row, *plan)
    for k in range(4):
        inputs, upstream = pick((own, right, left, over_in, over_up), k)
        n = inputs.shape[0]
        s = slice(k * n, (k + 1) * n)
        inv_rms, inner = rows_of(every, k, n, hid, inputs.shape[1], pay_ref)
        d_normed = contract(pay_ref[1, s, :hid], gate[...], 1, 0) + contract(
            pay_ref[2, s, :hid], up[...], 1, 0
        )
        unit = inputs.astype(F32) * inv_rms
        gain_term = gain_term + jnp.sum(d_normed * unit, axis=0, keepdims=True)
        term = inv_rms * (gain_wide * d_normed - unit * (inner / features))
        term_ref[s, :] = term.astype(BF16)
        column = lax.broadcasted_iota(jnp.int32, (own_rows, n), 1) + k * n
        hot = jnp.where(index == column, 1.0, 0.0).astype(BF16)
        own_total = own_total + contract(hot, upstream, 1, 0)
    up_own[...] = own_total.astype(BF16)
    gain_hi = gain_term.astype(BF16).astype(F32)
    rows = plan[0] * plan[1] // nx
    extra = out.shape[1] - rows
    row = lax.broadcasted_iota(jnp.int32, (extra, gain_term.shape[1]), 0)
    extras = jnp.where(row == 0, gain_hi, jnp.where(row == 1, gain_term - gain_hi, 0.0)).astype(BF16)
    live = term_ref.shape[0]
    column = lax.broadcasted_iota(jnp.int32, (rows, live), 1)
    i = lax.broadcasted_iota(jnp.int32, (rows, 1), 0)
    for q in range(nx):
        row = (((i >> log2(own_rows)) * nx + q) << log2(own_rows)) + (i & (own_rows - 1))
        hot = jnp.where(where_packed(nums, row, *plan) == column, 1.0, 0.0).astype(BF16)
        out[q, :rows, :] = contract(hot, term_ref[...], 1, 0).astype(BF16)
        out[q, rows:, :] = extras


def grads_kernel(
    hid, own, right, left, over_in, over_up, every, gain,
    grad_gate, grad_up, grad_down, pay_ref, normed_ref, up_ref,
):
    gain_wide = gain[...].astype(F32)
    for k in range(4):
        inputs, upstream = pick((own, right, left, over_in, over_up), k)
        n = inputs.shape[0]
        s = slice(k * n, (k + 1) * n)
        inv_rms, _ = rows_of(every, k, n, hid, inputs.shape[1], pay_ref)
        normed_ref[s, :] = (inputs.astype(F32) * inv_rms * gain_wide).astype(BF16)
        up_ref[s, :] = upstream
    grad_down[...] = contract(pay_ref[0, :, :hid], up_ref[...], 0, 0).astype(BF16)
    normed = normed_ref[...]
    grad_gate[...] = contract(pay_ref[1, :, :hid], normed, 0, 0).astype(BF16)
    grad_up[...] = contract(pay_ref[2, :, :hid], normed, 0, 0).astype(BF16)


def middle_kernel(parts, out):
    sections, own_rows, lanes = out.shape
    width = parts.shape[2]
    rows = sections * own_rows
    total = parts[0].astype(F32)
    for r in range(1, parts.shape[0]):
        total = total + parts[r].astype(F32)
    out[:, :, :width] = total[:rows].astype(BF16).reshape(sections, own_rows, width)
    gain = total[rows : rows + 1] + total[rows + 1 : rows + 2]
    row = lax.broadcasted_iota(jnp.int32, (own_rows, 128), 0)
    tile = jnp.zeros((own_rows, 128), F32)
    for i in range(width // 128):
        tile = jnp.where(row == i, gain[:, i * 128 : (i + 1) * 128], tile)
    tile = tile.astype(BF16)
    for s in range(sections):
        out[s, :, width:] = tile


def final_kernel(parts, up_own, d_input, grad_gain):
    width = up_own.shape[1]
    total = parts[0].astype(F32)
    for r in range(1, parts.shape[0]):
        total = total + parts[r].astype(F32)
    d_input[...] = (up_own[...].astype(F32) + total[:, :width]).astype(BF16)
    for i in range(width // 128):
        grad_gain[:, i * 128 : (i + 1) * 128] = total[i : i + 1, width:]


def per_device(
    act_log, grad_log, failed_section, live_tokens, gate_weight, up_weight, down_weight, norm_gain
):
    ny, nzh, nx = (lax.axis_size(a) for a in ROWS_AXES)
    nzl, nc = lax.axis_size("zl"), lax.axis_size("c")
    sections = ny * nzh
    shards = sections * nx
    tokens, width = act_log.shape[1:]
    batches = live_tokens.shape[0]
    rows = batches * tokens
    live = 3 * rows // 4
    per = tokens // (ny * nx)
    cycles = live // tokens
    features = float(width * nzl * nc)
    hid = gate_weight.shape[1]
    failed = failed_section[0]
    source = (failed + sections - 1) % sections
    target = (failed + 1) % sections
    batch = jnp.arange(batches, dtype=jnp.int32)
    offs = jnp.sum(jnp.where(batch[None, :] < batch[:, None], live_tokens[None, :], 0), axis=1)
    x = lax.axis_index("x")
    me = lax.axis_index(ROWS_AXES)
    plan = (batches, tokens, per, nx, cycles * per, ny * cycles * per)

    def shape(*dims, dtype=BF16):
        return jax.ShapeDtypeStruct(dims, dtype)

    nums = jnp.stack([lax.axis_index("c"), x, me, lax.axis_index("zl")]).astype(jnp.int32)
    nums = jnp.concatenate([nums, live_tokens, offs.astype(jnp.int32)])
    send = call(
        functools.partial(scatter_kernel, per), shape(2 * tokens, width), [],
        4 * tokens * tokens * width, live_tokens, act_log, grad_log,
    )
    recv = lax.all_to_all(send, ("y", "x"), 0, 0, tiled=True).reshape(ny * nx, 2 * per, width)
    got = jnp.stack(
        [
            lax.dynamic_slice_in_dim(recv, source // nzh * nx, nx, 0)[:, :per],
            lax.dynamic_slice_in_dim(recv, target // nzh * nx, nx, 0)[:, per:],
        ]
    )
    place = lax.axis_index(("y", "x")) * per + jnp.arange(per, dtype=jnp.int32)
    slot = (place[None, :] - offs[:, None]) % tokens
    cycle = (offs[:, None] + slot) // tokens
    hit = (slot < live_tokens[:, None])[:, None, :] & (
        cycle[:, None, :] == jnp.arange(cycles, dtype=jnp.int32)[None, :, None]
    )
    packed = jnp.sum(
        jnp.where(hit[None, :, :, :, None], got[:, :, None].astype(F32), 0.0), axis=1
    ).astype(BF16)
    block = cycles * per
    packed = packed.reshape(2 * block, width)

    other = lax.ppermute(packed, "zh", [(0, 1), (1, 0)])
    packed = jnp.where(lax.axis_index("zh") == source % nzh, packed, other)

    copies = jnp.broadcast_to(packed[None], (ny,) + packed.shape).reshape(-1, width)
    column = lax.all_to_all(copies, "y", 0, 0, tiled=True)
    part = ny * block
    out_row = lax.broadcasted_iota(jnp.int32, (2 * part, 2 * part), 0)
    from_row = lax.broadcasted_iota(jnp.int32, (2 * part, 2 * part), 1)
    at = out_row % part
    hot = (at // block * 2 + out_row // part) * block + at % block == from_row
    own = contract(hot.astype(BF16), column, 1, 0).astype(BF16).reshape(2, part, width)
    forth = [(i, (i + 1) % nx) for i in range(nx)]
    back = [(i, (i - 1) % nx) for i in range(nx)]
    right = lax.ppermute(own, "x", forth)
    left = lax.ppermute(own, "x", back)
    over_in = lax.ppermute(right[0], "x", forth)
    over_up = lax.ppermute(left[1], "x", back)
    blocks = (own, right, left, over_in, over_up)

    inside = width - 2 * hid
    gate_rows, up_rows = gate_weight.T, up_weight.T
    ahead_rows = jnp.concatenate([gate_rows, up_rows, jnp.zeros((inside, width), BF16)], axis=0)
    behind_rows = jnp.concatenate([jnp.zeros((2 * hid, width), BF16), down_weight[:inside]], axis=0)
    rest_rows = down_weight[inside:]
    gain = norm_gain.reshape(1, width)
    own_count = live // nc // nzl
    size = own_count * (width // 128) + TAIL
    product = 2 * live * width * WIDE
    two = shape(2, size, 128)
    weights = (gain, ahead_rows, behind_rows, rest_rows)
    tail_ref = pltpu.VMEM((part, 128), F32)
    swap = [(0, 1), (1, 0)]
    keep_a, give_a, middle = call(
        early_kernel, (two,) * 3, [tail_ref] * 3, 4 * product, nums, own, right, left, *weights
    )
    taken_a = lax.ppermute(give_a, "c", swap)
    keep_b, give_b = call(
        late_kernel, (two,) * 2, [tail_ref], product, nums, middle, over_in, over_up, *weights
    )
    taken_b = lax.ppermute(give_b, "c", swap)
    chunk = shape(size, 128)
    pairs = call(pair_kernel, (chunk,) * nzl, [], nzl * size * 128, nums, keep_a, keep_b, taken_a, taken_b)
    others = [
        lax.ppermute(pairs[i], "zl", [(a, a ^ i) for a in range(nzl)]) for i in range(1, nzl)
    ]
    point = call(
        functools.partial(point_kernel, hid, features), chunk,
        [
            pltpu.VMEM((own_count, width), F32),
            pltpu.VMEM((own_count, hid), F32),
            pltpu.VMEM((128, 128), F32),
        ],
        20 * size * 128, pairs[0], *others,
    )
    every = lax.all_gather(point, ("zl", "c"), axis=0, tiled=True)

    own_rows = rows // shards
    count = rows // nx
    out, up_own = call(
        functools.partial(term_kernel, hid, features, plan),
        (shape(nx, count + 16, width), shape(own_rows, width)),
        [pltpu.VMEM((live, width), BF16), pltpu.VMEM((3, live, WIDE), BF16)],
        5 * product,
        nums, *blocks, every, gain, gate_rows, up_rows,
    )
    out = lax.all_to_all(out, "x", 0, 0, tiled=True)
    out = call(
        middle_kernel, shape(sections, own_rows, width + 128), [], nx * count * width, out
    )
    out = lax.all_to_all(out, ("y", "zh"), 0, 0, tiled=True)
    d_input, grad_gain = call(
        final_kernel, (shape(own_rows, width), shape(1, width, dtype=F32)), [],
        sections * own_rows * width, out, up_own,
    )

    grad_gate, grad_up, grad_down = call(
        functools.partial(grads_kernel, hid),
        (shape(hid, width),) * 3,
        [
            pltpu.VMEM((3, live, WIDE), BF16),
            pltpu.VMEM((live, width), BF16),
            pltpu.VMEM((live, width), BF16),
        ],
        3 * product,
        *blocks, every, gain,
    )
    return (d_input, grad_gate.T, grad_up.T, grad_down, grad_gain.reshape(width))


def solution(mesh):
    fine = Mesh(mesh.devices.reshape(8, 2, 4, 4, 2), AXES)
    section, replica, tensor = ("y", "zh"), "x", ("zl", "c")
    split = ("y", "zh", "x")
    in_specs = (
        P(section, replica, tensor),
        P(section, replica, tensor),
        P(),
        P(),
        P(tensor, split),
        P(tensor, split),
        P(split, tensor),
        P(tensor),
    )
    out_specs = (
        P(split, tensor),
        P(tensor, split),
        P(tensor, split),
        P(split, tensor),
        P(tensor),
    )
    return jax.shard_map(
        per_device, mesh=fine, in_specs=in_specs, out_specs=out_specs, check_vma=False
    )
```
